256 devices in a mesh: sta: 32 (over x, z_lo, core), day: 8 (over y, z_hi).
Axes of the slice: x: 4, y: 4, z: 8 (z_hi: 2, z_lo: 4; z = z_hi * 4 + z_lo), core: 2. Of those that a mesh axis runs over, the one named last changes fastest.
Arguments:
- spectra: bfloat16 [32, 2, 32, 3, 1536], P('sta', None, 'day'), may hold values from -1600 to 1600
- flags: int32 [32, 32], P('sta', 'day'), may hold values from 0 to 1
- pair_mask: int32 [32, 32], P('sta'), may hold values 0 or 1
Outputs:
- hourly: bfloat16 [8, 9, 32, 32, 256], P('day', None, 'sta')
- reference_stack: float32 [9, 32, 32, 256], P(None, 'sta', 'day')
The draws below stay inside these ranges and needn't reach their ends.
All inputs are finite; a program needn't handle non-finite values. No bound on the sum of `pair_mask` on one device may be relied on, other than what follows from the above.
Results may differ from the reference program's by a relative error of at most 0.017.
Values may be sent and summed in bfloat16 or wider, within the bound.
A program may use at most 64 MiB of HBM per device.

```python
import math
import jax
import jax.numpy as jnp
from jax import lax

F = 1536
LAGS = 256
COMPS = 3
HALF_BAND = 16
STA_DEV = 1
WIN_DEV = 4
STATIONS = 32
WINDOWS = 32
N_STA = 32
N_DAY = 8


def draw_spectra(key, part):
    key = jax.random.fold_in(key, 11)
    key_base, key_bins, key_level = jax.random.split(key, 3)
    shape_full = (STATIONS, 2, WINDOWS, COMPS, F)
    base = jnp.clip(jax.random.normal(key_base, shape_full, jnp.float32), -6.0, 6.0)
    top = math.log(10.0)
    rough = jnp.exp(jax.random.uniform(key_bins, (STATIONS, 1, 1, 1, F), jnp.float32) * top)
    level = jnp.exp(jax.random.uniform(key_level, (STATIONS, 1, WINDOWS, 1, 1), jnp.float32) * top)
    return (base * rough * level).astype(jnp.bfloat16)


def draw_flags(key, part):
    key = jax.random.fold_in(key, 23)
    key_level, key_roll = jax.random.split(key, 2)
    station_level = jax.random.randint(key_level, (STATIONS, 1), 0, 5)
    window_roll = jax.random.randint(key_roll, (STATIONS, WINDOWS), 0, 4)
    return (window_roll < station_level).astype(jnp.int32)


def touch_ends(values, stream_key, smallest, top_value):
    dims = values.shape
    place = [jax.random.randint(jax.random.fold_in(stream_key, axis), (), 0, dims[axis]) for axis in range(len(dims))]
    values = values.at[tuple(place)].set(smallest)
    longest = dims.index(max(dims))
    place[longest] = (place[longest] + 1) % dims[longest]
    return values.at[tuple(place)].set(top_value)


def setup_inputs(seed: int = 0) -> dict:
    streams_of = jax.random.split(jax.random.key(seed), 4)
    spectra = draw_spectra(jax.random.fold_in(streams_of[3], 71), 0)
    flags = draw_flags(jax.random.fold_in(streams_of[3], 71), 0)
    pair_mask = touch_ends((jax.random.randint(streams_of[2], (STATIONS, STATIONS), 0, 4) < 3).astype(jnp.int32), jax.random.fold_in(streams_of[2], 1), 0, 1)
    return dict(spectra=spectra, flags=flags, pair_mask=pair_mask)


def whiten(spectra, flags):
    values = spectra.astype(jnp.float32)
    bins_count = values.shape[-1]
    power_sum = lax.optimization_barrier(jnp.sum(values * values, axis=(1, 3)))
    padded = jnp.pad(power_sum, ((0, 0), (0, 0), (HALF_BAND, HALF_BAND)))
    smooth = padded[:, :, 0:bins_count]
    for shift_bins in range(1, 2 * HALF_BAND + 1):
        smooth = smooth + padded[:, :, shift_bins:shift_bins + bins_count]
    root_mean = jnp.sqrt(smooth / (6.0 * (2 * HALF_BAND + 1)) + 1e-06)
    good_flags = (1 - flags).astype(jnp.bfloat16)
    scaling = good_flags.astype(jnp.float32)[:, None, :, None, None] / root_mean[:, None, :, None, :]
    return ((values * scaling).astype(jnp.bfloat16), good_flags)

def lag_table(bins_count, lag_count):
    freq_index = jnp.arange(bins_count, dtype=jnp.int32)
    lag_index = jnp.arange(lag_count, dtype=jnp.int32) - lag_count // 2
    phase_step = freq_index[:, None] * lag_index[None, :] % (2 * bins_count)
    phase_angle = phase_step.astype(jnp.float32) * (math.pi / bins_count)
    return jnp.concatenate([jnp.cos(phase_angle), -jnp.sin(phase_angle)], axis=0).astype(jnp.bfloat16)

def contract(first, second):
    return jnp.einsum('swaf,twbf->abstf', first.astype(jnp.float32), second.astype(jnp.float32))

def block_correlate(local_block, whole_day, table_float):
    bins_count = local_block.shape[-1]
    real_part = contract(local_block[:, 0], whole_day[:, 0]) + contract(local_block[:, 1], whole_day[:, 1])
    imag_part = contract(local_block[:, 1], whole_day[:, 0]) - contract(local_block[:, 0], whole_day[:, 1])
    stacked = jnp.concatenate([real_part.astype(jnp.bfloat16), imag_part.astype(jnp.bfloat16)], axis=-1)
    stacked = lax.optimization_barrier(stacked).astype(jnp.float32)
    rows_here = local_block.shape[0]
    others = whole_day.shape[0]
    flat = stacked.reshape(-1, 2 * bins_count)
    result = jnp.dot(flat, table_float, preferred_element_type=jnp.float32) * (1.0 / math.sqrt(bins_count))
    return result.reshape(9, rows_here, others, table_float.shape[1])

def reference(spectra, flags, pair_mask):
    whitened, good_flags = whiten(spectra, flags)
    table_float = lag_table(F, LAGS).astype(jnp.float32)
    mask_float = pair_mask.astype(jnp.float32)[None, :, :, None]
    running = jnp.zeros((9, STATIONS, STATIONS, LAGS), jnp.float32)
    count_sum = jnp.zeros((STATIONS, STATIONS), jnp.float32)
    hourly_list = []
    for day_index in range(N_DAY):
        day_whit = whitened[:, :, day_index * WIN_DEV:(day_index + 1) * WIN_DEV]
        day_good = good_flags[:, day_index * WIN_DEV:(day_index + 1) * WIN_DEV]
        blocks = day_whit.reshape(N_STA, STA_DEV, 2, WIN_DEV, COMPS, F)

        def one_block(local_block):
            return block_correlate(local_block, day_whit, table_float)
        correlation = lax.map(one_block, blocks)
        correlation = jnp.transpose(correlation, (1, 0, 2, 3, 4)).reshape(9, STATIONS, STATIONS, LAGS)
        pair_counts = jnp.dot(day_good, day_good.T, preferred_element_type=jnp.float32)
        hourly_list.append((mask_float * correlation / jnp.maximum(pair_counts, 1.0)[None, :, :, None]).astype(jnp.bfloat16))
        rounded = lax.optimization_barrier(correlation.astype(jnp.bfloat16)).astype(jnp.float32)
        running = running + rounded
        count_sum = count_sum + pair_counts
    reference_stack = mask_float * running / jnp.maximum(count_sum, 1.0)[None, :, :, None]
    return (jnp.stack(hourly_list), reference_stack)
```

```python
import math

import jax
import jax.numpy as jnp
import ml_dtypes
import numpy as np
from jax import lax
from jax.experimental import pallas as pl
from jax.experimental.pallas import tpu as pltpu
from jax.sharding import PartitionSpec as P

BINS = 1536
LAGS = 256
HALF_BAND = 16
WIN = 4
LANES = 128
FC = BINS // LANES
ROWS_FC = 24
FLAG_ROWS = 16
ROWS = FLAG_ROWS + FC * ROWS_FC
NC = 3
FCC = FC // NC
BOUNDS = [0] + [FLAG_ROWS + (k + 1) * FCC * ROWS_FC for k in range(NC)]
PAD = 128
MESH = pl.DeviceIdType.MESH


def lag_table():
    freq = np.arange(BINS, dtype=np.int64)
    lag = np.arange(LAGS, dtype=np.int64) - LAGS // 2
    angle = (freq[:, None] * lag[None, :] % (2 * BINS)) * (math.pi / BINS)
    parts = np.stack([np.cos(angle), -np.sin(angle)]).reshape(2, FC, LANES, LAGS)
    rows = np.transpose(parts, (1, 0, 2, 3)).reshape(2 * BINS, LAGS)
    return rows.astype(np.float32).astype(ml_dtypes.bfloat16)


def kernel(
    spec_ref, flags_ref, mask_ref, table_hbm,
    hourly_ref, stack_ref,
    power, white, t_blocks, s_blocks, t_wide, s_wide, table, products, total,
    mask_col, wide, hour_send, hour_recv, ref_send, ref_recv, hour_wide,
    table_sem, zs, zr, xs, xr, cs, cr, hs, hr, rs, rr,
):
    sta = lax.axis_index("sta")
    day = lax.axis_index("day")
    x0, z0, c0 = sta // 8, (sta // 2) % 4, sta % 2
    y0, h0 = day // 2, day % 2

    def sta_of(x, z, c):
        return (x * 4 + z) * 2 + c

    def at(x, z, c, d):
        return (sta_of(x, z, c), d)

    sibling = at(x0, z0, 1 - c0, day)

    barrier = pltpu.get_barrier_semaphore()

    def greet(target):
        pl.semaphore_signal(barrier, inc=1, device_id=target, device_id_type=MESH)

    for step in (1, 2, 3):
        greet(at((x0 + step) % 4, z0, c0, day))
        greet(at(x0, (z0 + step) % 4, c0, day))
    greet(sibling)
    mine = x0 == y0
    for d in range(8):

        @pl.when(jnp.logical_not(jnp.logical_and(mine, d == day)))
        def _():
            greet(at(y0, z0, c0, d))

    table_copy = pltpu.make_async_copy(table_hbm, table, table_sem)
    table_copy.start()

    power[...] = jnp.zeros_like(power)
    for w in range(WIN):
        re = spec_ref[0, 0, w].astype(jnp.float32)
        im = spec_ref[0, 1, w].astype(jnp.float32)
        q = re * re + im * im
        power[w : w + 1, 0:BINS] = q[0:1] + q[1:2] + q[2:3]
    single = power[...]
    span = single
    for shift in (1, 2, 4, 8, 16):
        span = span + pltpu.roll(span, shift, axis=1)
    span = span + pltpu.roll(single, 2 * HALF_BAND, axis=1)
    smooth = pltpu.roll(span, BINS + PAD - HALF_BAND, axis=1)[:, 0:BINS]
    scale = lax.rsqrt(smooth / (6.0 * (2 * HALF_BAND + 1)) + 1e-06)
    for w in range(WIN):
        good = (1 - flags_ref[0, w]).astype(jnp.float32)
        row = scale[w : w + 1] * good
        for part in range(2):
            y = spec_ref[0, part, w].astype(jnp.float32) * row
            first = FLAG_ROWS + (part * WIN + w) * 3
            for fc in range(FC):
                white[first + fc * ROWS_FC : first + fc * ROWS_FC + 3, :] = y[
                    :, fc * LANES : (fc + 1) * LANES
                ]
        white[w : w + 1, :] = jnp.full((1, LANES), good)
    white[WIN:FLAG_ROWS, :] = jnp.zeros((FLAG_ROWS - WIN, LANES), jnp.float32)
    block = white[...].astype(jnp.bfloat16)
    own = z0 * 2 + c0
    t_blocks[own] = block
    s_blocks[x0] = block

    line = lax.broadcasted_iota(jnp.int32, (32, 32), 0)
    place = lax.broadcasted_iota(jnp.int32, (32, 32), 1)
    spread = jnp.broadcast_to(mask_ref[...].astype(jnp.float32), (32, 32))
    column = jnp.sum(jnp.where(line == place, spread, 0.0), axis=1, keepdims=True)
    mask_col[...] = jnp.broadcast_to(column, (32, LAGS))

    pl.semaphore_wait(barrier, 15 - mine.astype(jnp.int32))

    def piece(ref, slot, k):
        return ref.at[slot, pl.ds(BOUNDS[k], BOUNDS[k + 1] - BOUNDS[k]), :]

    def z_copy(step, k, slot):
        return pltpu.make_async_remote_copy(
            src_ref=piece(t_blocks, own, k),
            dst_ref=piece(t_blocks, slot, k),
            send_sem=zs.at[step, k],
            recv_sem=zr.at[step, k],
            device_id=at(x0, (z0 + step) % 4, c0, day),
            device_id_type=MESH,
        )

    def x_copy(step, k, slot):
        return pltpu.make_async_remote_copy(
            src_ref=piece(s_blocks, x0, k),
            dst_ref=piece(s_blocks, slot, k),
            send_sem=xs.at[step, k],
            recv_sem=xr.at[step, k],
            device_id=at((x0 + step) % 4, z0, c0, day),
            device_id_type=MESH,
        )

    def core_copy(step, k, core):
        slot = ((z0 - step + 4) % 4) * 2 + core
        return pltpu.make_async_remote_copy(
            src_ref=piece(t_blocks, slot, k),
            dst_ref=piece(t_blocks, slot, k),
            send_sem=cs.at[step, k],
            recv_sem=cr.at[step, k],
            device_id=sibling,
            device_id_type=MESH,
        )

    for k in range(NC):
        for step in (2, 1, 3):
            z_copy(step, k, own).start()
        for step in (2, 1, 3):
            x_copy(step, k, x0).start()
        core_copy(0, k, c0).start()

    table_copy.wait()
    for k in range(NC):
        for step in (1, 3, 2):
            z_copy(step, k, ((z0 - step + 4) % 4) * 2 + c0).wait_recv()
            core_copy(step, k, c0).start()
        for step in (1, 3, 2):
            x_copy(step, k, (x0 - step + 4) % 4).wait_recv()
        for step in range(4):
            core_copy(step, k, 1 - c0).wait_recv()
        low, high = BOUNDS[k], BOUNDS[k + 1]
        for slot in range(8):
            t_wide[slot * ROWS + low : slot * ROWS + high, :] = t_blocks[slot, low:high].astype(
                jnp.float32
            )
        for slot in range(4):
            s_wide[slot * ROWS + low : slot * ROWS + high, :] = s_blocks[slot, low:high].astype(
                jnp.float32
            )

        def cross(i, carry):
            fc = k * FCC + i
            base = FLAG_ROWS + fc * ROWS_FC
            t = [t_wide[pl.ds(base + r, 8, stride=ROWS), :] for r in range(ROWS_FC)]
            column = pl.multiple_of(fc * 2 * LANES, 2 * LANES)
            for pair in range(6):
                re_tiles, im_tiles = [], []
                for sa in (2 * pair, 2 * pair + 1):
                    s, a = divmod(sa, 3)
                    local = [
                        jnp.broadcast_to(
                            s_wide[pl.ds(s * ROWS + base + r * 3 + a, 1), :], (8, LANES)
                        )
                        for r in range(2 * WIN)
                    ]
                    for b in range(3):
                        re, im = None, None
                        for w in range(WIN):
                            t_re, t_im = t[w * 3 + b], t[(WIN + w) * 3 + b]
                            re_term = local[w] * t_re + local[WIN + w] * t_im
                            im_term = local[WIN + w] * t_re - local[w] * t_im
                            re = re_term if re is None else re + re_term
                            im = im_term if im is None else im + im_term
                        re_tiles.append(re)
                        im_tiles.append(im)
                rows = pl.ds(pair * 48, 48)
                products[rows, pl.ds(column, LANES)] = jnp.concatenate(re_tiles, axis=0).astype(
                    jnp.bfloat16
                )
                products[rows, pl.ds(column + LANES, LANES)] = jnp.concatenate(
                    im_tiles, axis=0
                ).astype(jnp.bfloat16)
            return carry

        lax.fori_loop(0, FCC, cross, 0)
        depth = FCC * 2 * LANES
        term = jnp.dot(
            products[:, k * depth : (k + 1) * depth],
            table[k * depth : (k + 1) * depth, :],
            preferred_element_type=jnp.float32,
        )
        total[...] = term if k == 0 else total[...] + term

    def hour_copy(step, slot):
        return pltpu.make_async_remote_copy(
            src_ref=hour_send.at[step],
            dst_ref=hour_recv.at[slot],
            send_sem=hs.at[step],
            recv_sem=hr.at[step],
            device_id=at((x0 + step) % 4, z0, c0, day),
            device_id_type=MESH,
        )

    def ref_copy(step, other, slot):
        return pltpu.make_async_remote_copy(
            src_ref=ref_send.at[step, other],
            dst_ref=ref_recv.at[slot],
            send_sem=rs.at[step, other],
            recv_sem=rr.at[slot],
            device_id=at((x0 + step) % 4, z0, c0, x0 * 2 + (h0 + other) % 2),
            device_id_type=MESH,
        )

    for step in (2, 1, 3, 0):
        s = (x0 + step) % 4
        first = pl.multiple_of(s * 72, 8)
        first_s = pl.multiple_of(s * ROWS, 8)
        count = None
        for w in range(WIN):
            g = s_wide[pl.ds(first_s + w, 1), :] * t_wide[pl.ds(w, 8, stride=ROWS), :]
            count = g if count is None else count + g
        whole = jnp.concatenate(
            [
                total[pl.ds(first, 72), :] * (1.0 / math.sqrt(BINS)),
                jnp.concatenate([count, count], axis=1),
            ],
            axis=0,
        )
        for side in range(2):
            for half in range(2):
                for p in range(10):
                    wide[side, half * 40 + p * 4 : half * 40 + p * 4 + 4, :] = whole[
                        p * 8 + side * 4 : p * 8 + side * 4 + 4, half * LANES : (half + 1) * LANES
                    ]
        for other in range(2):
            ref_send[step, other] = wide[(h0 + other) % 2].astype(jnp.bfloat16)
        if step == 0:
            hour_recv[x0] = whole.astype(jnp.bfloat16)

            @pl.when(mine)
            def _():
                ref_recv[day] = ref_send[0, 0]

            @pl.when(jnp.logical_not(mine))
            def _():
                ref_copy(0, 0, day).start()

            ref_copy(0, 1, day).start()
        else:
            hour_send[step] = whole.astype(jnp.bfloat16)
            for other in (1, 0):
                ref_copy(step, other, day).start()
            hour_copy(step, x0).start()

    for step in (0, 1, 3, 2):
        x = (x0 - step + 4) % 4
        if step:
            hour_copy(step, x).wait_recv()
        got = hour_recv[x].astype(jnp.float32)
        rows = pl.ds(pl.multiple_of(x * 8, 8), 8)
        factor = mask_col[rows, :] / jnp.maximum(got[72:80], 1.0)
        for p in range(9):
            hour_wide[p, rows, :] = got[p * 8 : p * 8 + 8] * factor
    for p in range(9):
        hourly_ref[0, p, 0] = hour_wide[p].astype(jnp.bfloat16)

    for d in range(8):

        @pl.when(jnp.logical_not(jnp.logical_and(mine, d == day)))
        def _():
            ref_copy(1, 0, d).wait_recv()

    summed = ref_recv[0].astype(jnp.float32)
    for d in range(1, 8):
        summed = summed + ref_recv[d].astype(jnp.float32)
    mask8 = mask_col[pl.ds(pl.multiple_of(y0 * 8, 8), 8), 0:LANES]
    mask4 = jnp.where(h0 == 0, mask8[0:4], mask8[4:8])
    for half in range(2):
        part = summed[half * 40 : half * 40 + 40]
        factor = mask4 / jnp.maximum(part[36:40], 1.0)
        for p in range(9):
            stack_ref[p, 0, :, half * LANES : (half + 1) * LANES] = part[p * 4 : p * 4 + 4] * factor

    for k in range(NC):
        for step in (1, 2, 3):
            z_copy(step, k, own).wait_send()
            x_copy(step, k, x0).wait_send()
        for step in range(4):
            core_copy(step, k, c0).wait_send()
    for step in range(4):
        if step:
            hour_copy(step, x0).wait_send()
            ref_copy(step, 0, day).wait_send()
        else:

            @pl.when(jnp.logical_not(mine))
            def _():
                ref_copy(0, 0, day).wait_send()

        ref_copy(step, 1, day).wait_send()


def on_device(spectra, flags, pair_mask):
    table = jnp.asarray(lag_table())
    bf16, f32 = jnp.bfloat16, jnp.float32
    dma = pltpu.SemaphoreType.DMA
    vmem = pltpu.VMEM
    return pl.pallas_call(
        kernel,
        out_shape=(
            jax.ShapeDtypeStruct((1, 9, 1, 32, LAGS), bf16),
            jax.ShapeDtypeStruct((9, 1, 4, LAGS), f32),
        ),
        in_specs=[
            pl.BlockSpec(memory_space=pltpu.VMEM),
            pl.BlockSpec(memory_space=pltpu.SMEM),
            pl.BlockSpec(memory_space=pltpu.VMEM),
            pl.BlockSpec(memory_space=pl.ANY),
        ],
        out_specs=(
            pl.BlockSpec(memory_space=pltpu.VMEM),
            pl.BlockSpec(memory_space=pltpu.VMEM),
        ),
        scratch_shapes=[
            vmem((8, BINS + PAD), f32),
            vmem((ROWS, LANES), f32),
            vmem((8, ROWS, LANES), bf16),
            vmem((4, ROWS, LANES), bf16),
            vmem((8 * ROWS, LANES), f32),
            vmem((4 * ROWS, LANES), f32),
            vmem((2 * BINS, LAGS), bf16),
            vmem((288, 2 * BINS), bf16),
            vmem((288, LAGS), f32),
            vmem((32, LAGS), f32),
            vmem((2, 80, LANES), f32),
            vmem((4, 80, LAGS), bf16),
            vmem((4, 80, LAGS), bf16),
            vmem((4, 2, 80, LANES), bf16),
            vmem((8, 80, LANES), bf16),
            vmem((9, 32, LAGS), f32),
            dma,
            dma((4, NC)),
            dma((4, NC)),
            dma((4, NC)),
            dma((4, NC)),
            dma((4, NC)),
            dma((4, NC)),
            dma((4,)),
            dma((4,)),
            dma((4, 2)),
            dma((8,)),
        ],
        compiler_params=pltpu.CompilerParams(
            collective_id=0, has_side_effects=True, vmem_limit_bytes=32 * 1024 * 1024
        ),
        cost_estimate=pl.CostEstimate(
            flops=500_000_000, bytes_accessed=2_000_000, transcendentals=6144
        ),
    )(spectra, flags, pair_mask, table)


def solution(mesh):
    placed = (P("sta", None, "day", None, None), P("sta", "day"), P("sta", None))
    return jax.shard_map(
        on_device,
        mesh=mesh,
        in_specs=placed,
        out_specs=(P("day", None, "sta", None, None), P(None, "sta", "day", None)),
        check_vma=False,
    )
```

```python
import math

import jax
import jax.numpy as jnp
import ml_dtypes
import numpy as np
from jax import lax
from jax.experimental import pallas as pl
from jax.experimental.pallas import tpu as pltpu
from jax.sharding import PartitionSpec as P

BINS = 1536
LAGS = 256
HALF_BAND = 16
WIN = 4
LANES = 128
FC = BINS // LANES
ROWS_FC = 24
FLAG_ROWS = 16
ROWS = FLAG_ROWS + FC * ROWS_FC
NC = 3
FCC = FC // NC
BOUNDS = [0] + [FLAG_ROWS + (k + 1) * FCC * ROWS_FC for k in range(NC)]
PAD = 128
MESH = pl.DeviceIdType.MESH


def lag_table():
    freq = np.arange(BINS, dtype=np.int64)
    lag = np.arange(LAGS, dtype=np.int64) - LAGS // 2
    angle = (freq[:, None] * lag[None, :] % (2 * BINS)) * (math.pi / BINS)
    parts = np.stack([np.cos(angle), -np.sin(angle)]).reshape(2, FC, LANES, LAGS)
    rows = np.transpose(parts, (1, 0, 2, 3)).reshape(2 * BINS, LAGS)
    return rows.astype(np.float32).astype(ml_dtypes.bfloat16)


def kernel(
    spec_hbm, flags_hbm, mask_hbm, table_hbm,
    hourly_ref, stack_ref,
    spec_ref, flags_ref, mask_ref, power, white, t_blocks, s_blocks, t_wide, s_wide, table, products, total,
    mask_col, mask_own, wide, hour_send, hour_recv, ref_send, ref_recv, ref_wide,
    in_sems, table_sem, zs, zr, fs, xs, xr, cs, cr, hs, hr, rs, rr, ready,
):
    sta = lax.axis_index("sta")
    day = lax.axis_index("day")
    x0, z0, c0 = sta // 8, (sta // 2) % 4, sta % 2
    y0, h0 = day // 2, day % 2

    def sta_of(x, z, c):
        return (x * 4 + z) * 2 + c

    def at(x, z, c, d):
        return (sta_of(x, z, c), d)

    sibling = at(x0, z0, 1 - c0, day)

    loads = [
        pltpu.make_async_copy(spec_hbm, spec_ref, in_sems.at[0]),
        pltpu.make_async_copy(flags_hbm, flags_ref, in_sems.at[1]),
        pltpu.make_async_copy(mask_hbm, mask_ref, in_sems.at[2]),
    ]
    for load in loads:
        load.start()
    table_copy = pltpu.make_async_copy(table_hbm, table, table_sem)
    table_copy.start()

    barrier = pltpu.get_barrier_semaphore()

    def greet(target):
        pl.semaphore_signal(barrier, inc=1, device_id=target, device_id_type=MESH)

    for step in (1, 2, 3):
        greet(at((x0 + step) % 4, z0, c0, day))
        greet(at(x0, (z0 + step) % 4, c0, day))
    greet(sibling)
    mine = x0 == y0
    early = h0 == 0
    for y in range(4):

        @pl.when(jnp.logical_not(jnp.logical_and(mine, y == y0)))
        def _():
            greet(at(y0, z0, c0, y * 2 + h0))

        @pl.when(early)
        def _():
            greet(at(y0, z0, c0, y * 2 + 1))
            greet(at(y, z0, c0, x0 * 2 + 1))

    loads[0].wait()
    loads[1].wait()
    power[...] = jnp.zeros_like(power)
    energy = None
    for part in range(2):
        for comp in range(3):
            values = spec_ref[0, part, comp].astype(jnp.float32)
            energy = values * values if energy is None else energy + values * values
    power[0:WIN, 0:BINS] = energy
    single = power[...]
    span = single
    for shift in (1, 2, 4, 8, 16):
        span = span + pltpu.roll(span, shift, axis=1)
    span = span + pltpu.roll(single, 2 * HALF_BAND, axis=1)
    smooth = pltpu.roll(span, BINS + PAD - HALF_BAND, axis=1)[0:WIN, 0:BINS]
    line = lax.broadcasted_iota(jnp.int32, (WIN, WIN), 0)
    place = lax.broadcasted_iota(jnp.int32, (WIN, WIN), 1)
    spread = jnp.broadcast_to((1 - flags_ref[...]).astype(jnp.float32), (WIN, WIN))
    good = jnp.sum(jnp.where(line == place, spread, 0.0), axis=1, keepdims=True)
    scale = lax.rsqrt(smooth / (6.0 * (2 * HALF_BAND + 1)) + 1e-06) * good
    for part in range(2):
        for comp in range(3):
            y = spec_ref[0, part, comp].astype(jnp.float32) * scale
            first = FLAG_ROWS + (part * 3 + comp) * WIN
            for fc in range(FC):
                white[first + fc * ROWS_FC : first + fc * ROWS_FC + WIN, :] = y[
                    :, fc * LANES : (fc + 1) * LANES
                ]
    white[0:WIN, :] = jnp.broadcast_to(good, (WIN, LANES))
    white[WIN:FLAG_ROWS, :] = jnp.zeros((FLAG_ROWS - WIN, LANES), jnp.float32)
    block = white[...].astype(jnp.bfloat16)
    own = z0 * 2 + c0
    t_blocks[own] = block
    s_blocks[x0] = block

    loads[2].wait()
    spread = jnp.broadcast_to(mask_ref[...].astype(jnp.float32), (32, 32))
    line = lax.broadcasted_iota(jnp.int32, (32, 32), 0)
    place = lax.broadcasted_iota(jnp.int32, (32, 32), 1)
    column = jnp.sum(jnp.where(line == place, spread, 0.0), axis=1, keepdims=True)
    mask_col[...] = jnp.broadcast_to(column, (32, LANES))
    column = jnp.sum(
        jnp.where(line[0:8] + day * 4 == place[0:8], spread[0:8], 0.0), axis=1, keepdims=True
    )
    mask_own[...] = jnp.broadcast_to(column, (8, LANES))

    @pl.when(early)
    def _():
        pl.semaphore_wait(barrier, 11 - mine.astype(jnp.int32))

    @pl.when(jnp.logical_not(early))
    def _():
        pl.semaphore_wait(barrier, 19 - mine.astype(jnp.int32))
        for y in range(4):
            pl.semaphore_signal(
                ready, inc=1, device_id=at(y0, z0, c0, y * 2), device_id_type=MESH
            )


    def piece(ref, slot, k):
        return ref.at[slot, pl.ds(BOUNDS[k], BOUNDS[k + 1] - BOUNDS[k]), :]

    def z_copy(step, k, slot):
        return pltpu.make_async_remote_copy(
            src_ref=piece(t_blocks, own, k),
            dst_ref=piece(t_blocks, slot, k),
            send_sem=zs.at[step, k],
            recv_sem=zr.at[step, k],
            device_id=at(x0, (z0 + step) % 4, c0, day),
            device_id_type=MESH,
        )

    def relay(k, slot, z):
        return pltpu.make_async_remote_copy(
            src_ref=piece(t_blocks, slot, k),
            dst_ref=piece(t_blocks, slot, k),
            send_sem=fs.at[k],
            recv_sem=zr.at[2, k],
            device_id=at(x0, z, c0, day),
            device_id_type=MESH,
        )

    def x_copy(step, k, slot):
        return pltpu.make_async_remote_copy(
            src_ref=piece(s_blocks, x0, k),
            dst_ref=piece(s_blocks, slot, k),
            send_sem=xs.at[step, k],
            recv_sem=xr.at[step, k],
            device_id=at((x0 + step) % 4, z0, c0, day),
            device_id_type=MESH,
        )

    def core_copy(step, k, core):
        slot = ((z0 - step + 4) % 4) * 2 + core
        return pltpu.make_async_remote_copy(
            src_ref=piece(t_blocks, slot, k),
            dst_ref=piece(t_blocks, slot, k),
            send_sem=cs.at[step, k],
            recv_sem=cr.at[step, k],
            device_id=sibling,
            device_id_type=MESH,
        )

    outer = jnp.logical_or(z0 == 0, z0 == 3)
    inner = jnp.logical_not(outer)

    for k in range(NC):
        for step in (1, 3):
            z_copy(step, k, own).start()

        @pl.when(outer)
        def _():
            z_copy(2, k, own).start()

        for step in (2, 1, 3):
            x_copy(step, k, x0).start()
        core_copy(0, k, c0).start()

    table_copy.wait()
    for k in range(NC):

        @pl.when(z0 == 2)
        def _():
            z_copy(1, k, 2 + c0).wait_recv()
            relay(k, 2 + c0, 3).start()
            core_copy(1, k, c0).start()

        @pl.when(z0 == 1)
        def _():
            z_copy(3, k, 4 + c0).wait_recv()
            relay(k, 4 + c0, 0).start()
            core_copy(3, k, c0).start()

    for k in range(NC):
        @pl.when(z0 != 2)
        def _():
            z_copy(1, k, ((z0 + 3) % 4) * 2 + c0).wait_recv()
            core_copy(1, k, c0).start()

        @pl.when(z0 != 1)
        def _():
            z_copy(3, k, ((z0 + 1) % 4) * 2 + c0).wait_recv()
            core_copy(3, k, c0).start()

        z_copy(2, k, ((z0 + 2) % 4) * 2 + c0).wait_recv()
        core_copy(2, k, c0).start()
        for step in (1, 3, 2):
            x_copy(step, k, (x0 - step + 4) % 4).wait_recv()
        for step in range(4):
            core_copy(step, k, 1 - c0).wait_recv()
        low, high = BOUNDS[k], BOUNDS[k + 1]
        for slot in range(8):
            t_wide[slot * ROWS + low : slot * ROWS + high, :] = t_blocks[slot, low:high].astype(
                jnp.float32
            )
        for slot in range(4):
            s_wide[slot * ROWS + low : slot * ROWS + high, :] = s_blocks[slot, low:high].astype(
                jnp.float32
            )

        def cross(i, carry):
            fc = k * FCC + i
            base = FLAG_ROWS + fc * ROWS_FC
            t = [t_wide[pl.ds(base + r, 8, stride=ROWS), :] for r in range(ROWS_FC)]
            column = pl.multiple_of(fc * 2 * LANES, 2 * LANES)
            for pair in range(6):
                re_tiles, im_tiles = [], []
                for sa in (2 * pair, 2 * pair + 1):
                    s, a = divmod(sa, 3)
                    local = [
                        jnp.broadcast_to(
                            s_wide[pl.ds(s * ROWS + base + (part * 3 + a) * WIN + w, 1), :],
                            (8, LANES),
                        )
                        for part in range(2)
                        for w in range(WIN)
                    ]
                    for b in range(3):
                        re, im = None, None
                        for w in range(WIN):
                            t_re, t_im = t[b * WIN + w], t[(3 + b) * WIN + w]
                            re_term = local[w] * t_re + local[WIN + w] * t_im
                            im_term = local[WIN + w] * t_re - local[w] * t_im
                            re = re_term if re is None else re + re_term
                            im = im_term if im is None else im + im_term
                        re_tiles.append(re)
                        im_tiles.append(im)
                rows = pl.ds(pair * 48, 48)
                products[rows, pl.ds(column, LANES)] = jnp.concatenate(re_tiles, axis=0).astype(
                    jnp.bfloat16
                )
                products[rows, pl.ds(column + LANES, LANES)] = jnp.concatenate(
                    im_tiles, axis=0
                ).astype(jnp.bfloat16)
            return carry

        lax.fori_loop(0, FCC, cross, 0)
        depth = FCC * 2 * LANES
        term = jnp.dot(
            products[:, k * depth : (k + 1) * depth],
            table[k * depth : (k + 1) * depth, :],
            preferred_element_type=jnp.float32,
        )
        total[...] = term if k == 0 else total[...] + term

    def hour_copy(step, slot):
        return pltpu.make_async_remote_copy(
            src_ref=hour_send.at[step],
            dst_ref=hour_recv.at[slot],
            send_sem=hs.at[step],
            recv_sem=hr.at[step],
            device_id=at((x0 + step) % 4, z0, c0, day),
            device_id_type=MESH,
        )

    def ref_copy(step, h, slot):
        return pltpu.make_async_remote_copy(
            src_ref=ref_send.at[step, h],
            dst_ref=ref_recv.at[slot],
            send_sem=rs.at[step, h],
            recv_sem=rr.at[slot],
            device_id=at((x0 + step) % 4, z0, c0, x0 * 2 + h),
            device_id_type=MESH,
        )

    for step in (2, 1, 3, 0):
        x = (x0 + step) % 4
        first_s = pl.multiple_of(x * ROWS, 8)
        count = None
        for w in range(WIN):
            g = s_wide[pl.ds(first_s + w, 1), :] * t_wide[pl.ds(w, 8, stride=ROWS), :]
            count = g if count is None else count + g
        scaled = total[pl.ds(pl.multiple_of(x * 72, 8), 72), :] * (1.0 / math.sqrt(BINS))
        for half in range(2):
            first = step * 160 + half * 80
            wide[first : first + 72, :] = scaled[:, half * LANES : (half + 1) * LANES]
            wide[first + 72 : first + 80, :] = count
        for h in range(2):
            first = step * 160 + h * 4
            tiles = [
                wide[pl.ds(first + q * 64 + j, 8, stride=8), :] for j in range(4) for q in range(2)
            ] + [wide[pl.ds(first + 128 + j, 4, stride=8), :] for j in range(4)]
            ref_send[step, h] = jnp.concatenate(tiles, axis=0).astype(jnp.bfloat16)

        @pl.when(jnp.logical_not(early))
        def _():
            ref_copy(step, 0, day).start()

    def send_ref(step, h):
        if step:
            ref_copy(step, h, day).start()
        else:
            local = jnp.logical_and(mine, h0 == h)

            @pl.when(local)
            def _():
                ref_recv[day] = ref_send[0, h]

            @pl.when(jnp.logical_not(local))
            def _():
                ref_copy(0, h, day).start()

    @pl.when(early)
    def _():
        for step in (2, 1, 3, 0):
            send_ref(step, 0)

    @pl.when(jnp.logical_not(early))
    def _():
        for step in (2, 1, 3, 0):
            send_ref(step, 1)

    for step in (2, 1, 3, 0):
        message = wide[step * 160 : step * 160 + 160, :].astype(jnp.bfloat16)
        if step:
            hour_send[step] = message
            hour_copy(step, x0).start()
        else:
            hour_recv[x0] = message

    @pl.when(early)
    def _():
        pl.semaphore_wait(ready, 4)
        for step in (2, 1, 3, 0):
            ref_copy(step, 1, day).start()

    for step in (0, 1, 3, 2):
        x = (x0 - step + 4) % 4
        if step:
            hour_copy(step, x).wait_recv()
    for pair in range(2):
        for half in range(2):
            first = half * 80
            got = [
                hour_recv[pair * 2 + i, first : first + 80, :].astype(jnp.float32) for i in range(2)
            ]
            factors = [
                mask_col[pair * 16 + i * 8 : pair * 16 + i * 8 + 8, :]
                / jnp.maximum(got[i][72:80], 1.0)
                for i in range(2)
            ]
            for p in range(9):
                tiles = [got[i][p * 8 : p * 8 + 8] * factors[i] for i in range(2)]
                hourly_ref[
                    0, p, 0, pair * 16 : pair * 16 + 16, half * LANES : (half + 1) * LANES
                ] = jnp.concatenate(tiles, axis=0).astype(jnp.bfloat16)

    for d in range(8):

        @pl.when(jnp.logical_not(jnp.logical_and(mine, day == d)))
        def _():
            ref_copy(1, 0, d).wait_recv()

    summed = ref_recv[0].astype(jnp.float32)
    for d in range(1, 8):
        summed = summed + ref_recv[d].astype(jnp.float32)
    ref_wide[...] = summed

    def share(q):
        if q < 16:
            return ref_wide[pl.ds(q, 4, stride=16), :]
        return ref_wide[pl.ds(64 + q - 16, 4, stride=4), :]

    for half in range(2):
        factor = mask_own[0:4, :] / jnp.maximum(share(half * 10 + 9), 1.0)
        for p in range(9):
            stack_ref[p, 0, :, half * LANES : (half + 1) * LANES] = share(half * 10 + p) * factor

    for k in range(NC):
        for step in (1, 3):
            z_copy(step, k, own).wait_send()

        @pl.when(outer)
        def _():
            z_copy(2, k, own).wait_send()

        @pl.when(inner)
        def _():
            relay(k, own, z0).wait_send()

        for step in (1, 2, 3):
            x_copy(step, k, x0).wait_send()
        for step in range(4):
            core_copy(step, k, c0).wait_send()
    for step in (1, 2, 3):
        hour_copy(step, x0).wait_send()
        for h in range(2):
            ref_copy(step, h, day).wait_send()
    for h in range(2):

        @pl.when(jnp.logical_not(jnp.logical_and(mine, h0 == h)))
        def _():
            ref_copy(0, h, day).wait_send()


def on_device(spectra, flags, pair_mask):
    table = jnp.asarray(lag_table())
    bf16, f32 = jnp.bfloat16, jnp.float32
    dma = pltpu.SemaphoreType.DMA
    vmem = pltpu.VMEM
    operands = (jnp.transpose(spectra, (0, 1, 3, 2, 4)), flags, pair_mask, table)
    return pl.pallas_call(
        kernel,
        out_shape=(
            jax.ShapeDtypeStruct((1, 9, 1, 32, LAGS), bf16),
            jax.ShapeDtypeStruct((9, 1, 4, LAGS), f32),
        ),
        in_specs=[pl.BlockSpec(memory_space=pl.ANY)] * 4,
        out_specs=(
            pl.BlockSpec(memory_space=pltpu.VMEM),
            pl.BlockSpec(memory_space=pltpu.VMEM),
        ),
        scratch_shapes=[
            vmem((1, 2, 3, WIN, BINS), bf16),
            vmem((1, WIN), jnp.int32),
            vmem((1, 32), jnp.int32),
            vmem((8, BINS + PAD), f32),
            vmem((ROWS, LANES), f32),
            vmem((8, ROWS, LANES), bf16),
            vmem((4, ROWS, LANES), bf16),
            vmem((8 * ROWS, LANES), f32),
            vmem((4 * ROWS, LANES), f32),
            vmem((2 * BINS, LAGS), bf16),
            vmem((288, 2 * BINS), bf16),
            vmem((288, LAGS), f32),
            vmem((32, LANES), f32),
            vmem((8, LANES), f32),
            vmem((4 * 160, LANES), f32),
            vmem((4, 160, LANES), bf16),
            vmem((4, 160, LANES), bf16),
            vmem((4, 2, 80, LANES), bf16),
            vmem((8, 80, LANES), bf16),
            vmem((80, LANES), f32),
            dma((3,)),
            dma,
            dma((4, NC)),
            dma((4, NC)),
            dma((NC,)),
            dma((4, NC)),
            dma((4, NC)),
            dma((4, NC)),
            dma((4, NC)),
            dma((4,)),
            dma((4,)),
            dma((4, 2)),
            dma((8,)),
            pltpu.SemaphoreType.REGULAR,
        ],
        compiler_params=pltpu.CompilerParams(
            collective_id=0, has_side_effects=True, vmem_limit_bytes=32 * 1024 * 1024
        ),
        cost_estimate=pl.CostEstimate(
            flops=500_000_000, bytes_accessed=2_000_000, transcendentals=6144
        ),
    )(*(pltpu.with_memory_space_constraint(a, pltpu.HBM) for a in operands))


def solution(mesh):
    placed = (P("sta", None, "day", None, None), P("sta", "day"), P("sta", None))
    return jax.shard_map(
        on_device,
        mesh=mesh,
        in_specs=placed,
        out_specs=(P("day", None, "sta", None, None), P(None, "sta", "day", None)),
        check_vma=False,
    )
```

```python
import math

import jax
import jax.numpy as jnp
import ml_dtypes
import numpy as np
from jax import lax
from jax.experimental import pallas as pl
from jax.experimental.pallas import tpu as pltpu
from jax.sharding import PartitionSpec as P

BINS = 1536
LAGS = 256
HALF_BAND = 16
WIN = 4
LANES = 128
FC = BINS // LANES
ROWS_FC = 24
FLAG_ROWS = 16
ROWS = FLAG_ROWS + FC * ROWS_FC
BLOCK = 80
PAD = 128
MESH = pl.DeviceIdType.MESH


def lag_table():
    freq = np.arange(BINS, dtype=np.int64)
    lag = np.arange(LAGS, dtype=np.int64) - LAGS // 2
    angle = (freq[:, None] * lag[None, :] % (2 * BINS)) * (math.pi / BINS)
    parts = np.stack([np.cos(angle), -np.sin(angle)]).reshape(2, FC, LANES, LAGS)
    rows = np.transpose(parts, (1, 0, 2, 3)).reshape(2 * BINS, LAGS)
    return rows.astype(np.float32).astype(ml_dtypes.bfloat16)


def kernel(
    spec_hbm, flags_hbm, mask_hbm, table_hbm,
    hourly_ref, stack_ref,
    spec_ref, flags_ref, mask_ref, power, white, t_blocks, s_blocks, t_wide, s_wide, table, products, totals,
    mask_col, mask_own, result, hour_recv, ref_recv, hour_wide, hour_rest, ref_wide,
    in_sems, table_sem, zs, zr, fs, xs, xr, cs, cr, hs, hr, rs, rr, ready,
):
    sta = lax.axis_index("sta")
    day = lax.axis_index("day")
    x0, z0, c0 = sta // 8, (sta // 2) % 4, sta % 2
    y0, h0 = day // 2, day % 2

    def sta_of(x, z, c):
        return (x * 4 + z) * 2 + c

    def at(x, z, c, d):
        return (sta_of(x, z, c), d)

    sibling = at(x0, z0, 1 - c0, day)

    barrier = pltpu.get_barrier_semaphore()

    def greet(target):
        pl.semaphore_signal(barrier, inc=1, device_id=target, device_id_type=MESH)

    for step in (3, 1, 2):
        greet(at(x0, (z0 + step) % 4, c0, day))
    for step in (2, 1, 3):
        greet(at((x0 + step) % 4, z0, c0, day))
    greet(sibling)
    mine = x0 == y0
    early = h0 == 0
    for y in range(4):

        @pl.when(y != y0)
        def _():
            greet(at(x0, z0, c0, y * 2 + h0))

        @pl.when(early)
        def _():
            greet(at(y0, z0, c0, y * 2 + 1))
            greet(at(y, z0, c0, x0 * 2 + 1))

    loads = [
        pltpu.make_async_copy(spec_hbm, spec_ref, in_sems.at[0]),
        pltpu.make_async_copy(flags_hbm, flags_ref, in_sems.at[1]),
        pltpu.make_async_copy(mask_hbm, mask_ref, in_sems.at[2]),
    ]
    for load in loads:
        load.start()
    table_copy = pltpu.make_async_copy(table_hbm, table, table_sem)
    table_copy.start()

    loads[0].wait()
    loads[1].wait()
    power[...] = jnp.zeros_like(power)
    energy = None
    for part in range(2):
        for comp in range(3):
            values = spec_ref[0, part, comp].astype(jnp.float32)
            energy = values * values if energy is None else energy + values * values
    power[0:WIN, 0:BINS] = energy
    single = power[...]
    span = single
    for shift in (1, 2, 4, 8, 16):
        span = span + pltpu.roll(span, shift, axis=1)
    span = span + pltpu.roll(single, 2 * HALF_BAND, axis=1)
    smooth = pltpu.roll(span, BINS + PAD - HALF_BAND, axis=1)[0:WIN, 0:BINS]
    line = lax.broadcasted_iota(jnp.int32, (WIN, WIN), 0)
    place = lax.broadcasted_iota(jnp.int32, (WIN, WIN), 1)
    spread = jnp.broadcast_to((1 - flags_ref[...]).astype(jnp.float32), (WIN, WIN))
    good = jnp.sum(jnp.where(line == place, spread, 0.0), axis=1, keepdims=True)
    scale = lax.rsqrt(smooth / (6.0 * (2 * HALF_BAND + 1)) + 1e-06) * good
    for part in range(2):
        for comp in range(3):
            y = spec_ref[0, part, comp].astype(jnp.float32) * scale
            first = FLAG_ROWS + (part * 3 + comp) * WIN
            for fc in range(FC):
                white[first + fc * ROWS_FC : first + fc * ROWS_FC + WIN, :] = y[
                    :, fc * LANES : (fc + 1) * LANES
                ]
    white[0:WIN, :] = jnp.broadcast_to(good, (WIN, LANES))
    white[WIN:FLAG_ROWS, :] = jnp.zeros((FLAG_ROWS - WIN, LANES), jnp.float32)
    block = white[...].astype(jnp.bfloat16)
    own = z0 * 2 + c0
    t_blocks[own] = block
    s_blocks[x0] = block

    loads[2].wait()
    spread = jnp.broadcast_to(mask_ref[...].astype(jnp.float32), (32, 32))
    line = lax.broadcasted_iota(jnp.int32, (32, 32), 0)
    place = lax.broadcasted_iota(jnp.int32, (32, 32), 1)
    column = jnp.sum(jnp.where(line == place, spread, 0.0), axis=1, keepdims=True)
    mask_col[...] = jnp.broadcast_to(column, (32, LANES))
    column = jnp.sum(
        jnp.where(line[0:8] + day * 4 == place[0:8], spread[0:8], 0.0), axis=1, keepdims=True
    )
    mask_own[...] = jnp.broadcast_to(column, (8, LANES))

    @pl.when(early)
    def _():
        pl.semaphore_wait(barrier, 10)

    @pl.when(jnp.logical_not(early))
    def _():
        pl.semaphore_wait(barrier, 18)
        for y in range(4):
            pl.semaphore_signal(
                ready, inc=1, device_id=at(y0, z0, c0, y * 2), device_id_type=MESH
            )


    def z_copy(step, slot):
        return pltpu.make_async_remote_copy(
            src_ref=t_blocks.at[own],
            dst_ref=t_blocks.at[slot],
            send_sem=zs.at[step],
            recv_sem=zr.at[step],
            device_id=at(x0, (z0 + step) % 4, c0, day),
            device_id_type=MESH,
        )

    def relay(slot, z):
        return pltpu.make_async_remote_copy(
            src_ref=t_blocks.at[slot],
            dst_ref=t_blocks.at[slot],
            send_sem=fs,
            recv_sem=zr.at[2],
            device_id=at(x0, z, c0, day),
            device_id_type=MESH,
        )

    def x_copy(step, slot):
        return pltpu.make_async_remote_copy(
            src_ref=s_blocks.at[x0],
            dst_ref=s_blocks.at[slot],
            send_sem=xs.at[step],
            recv_sem=xr.at[step],
            device_id=at((x0 + step) % 4, z0, c0, day),
            device_id_type=MESH,
        )

    order = [z0, 1 + z0 % 2, 3 * (1 - z0 % 2), (z0 + 2) % 4]

    def core_copy(i, core):
        slot = order[i] * 2 + core
        return pltpu.make_async_remote_copy(
            src_ref=t_blocks.at[slot],
            dst_ref=t_blocks.at[slot],
            send_sem=cs.at[i],
            recv_sem=cr.at[i],
            device_id=sibling,
            device_id_type=MESH,
        )

    outer = jnp.logical_or(z0 == 0, z0 == 3)
    inner = jnp.logical_not(outer)

    @pl.when(z0 >= 2)
    def _():
        z_copy(1, own).start()
        z_copy(3, own).start()

    @pl.when(z0 < 2)
    def _():
        z_copy(3, own).start()
        z_copy(1, own).start()

    @pl.when(outer)
    def _():
        z_copy(2, own).start()

    for step in (2, 1, 3):
        x_copy(step, x0).start()
    core_copy(0, c0).start()

    def arrive(i):
        slot = order[i] * 2 + c0
        z_copy((z0 - order[i] + 4) % 4, slot).wait_recv()
        if i == 1:

            @pl.when(inner)
            def _():
                relay(slot, 3 * (z0 - 1)).start()

        core_copy(i, c0).start()

    high_rows = lax.broadcasted_iota(jnp.int32, (8, LANES), 0) >= 4

    def t_tile(row):
        first = jnp.broadcast_to(t_wide[pl.ds(row, 1), :], (8, LANES))
        second = jnp.broadcast_to(t_wide[pl.ds(ROWS + row, 1), :], (8, LANES))
        return jnp.where(high_rows, second, first)

    def s_tile(row):
        return s_wide[pl.ds(row, 8, stride=ROWS), :]

    def cross(i):
        for core in range(2):
            t_wide[core * ROWS : (core + 1) * ROWS, :] = t_blocks[order[i] * 2 + core].astype(
                jnp.float32
            )

        def chunk(fc, carry):
            base = FLAG_ROWS + fc * ROWS_FC
            local = [s_tile(base + r) for r in range(ROWS_FC)]
            column = pl.multiple_of(fc * 2 * LANES, 2 * LANES)
            re_tiles, im_tiles = [None] * 9, [None] * 9
            for b in range(3):
                other = [
                    t_tile(base + (part * 3 + b) * WIN + w) for part in range(2) for w in range(WIN)
                ]
                for a in range(3):
                    re, im = None, None
                    for w in range(WIN):
                        s_re, s_im = local[a * WIN + w], local[(3 + a) * WIN + w]
                        t_re, t_im = other[w], other[WIN + w]
                        re_term = s_re * t_re + s_im * t_im
                        im_term = s_im * t_re - s_re * t_im
                        re = re_term if re is None else re + re_term
                        im = im_term if im is None else im + im_term
                    re_tiles[a * 3 + b] = re
                    im_tiles[a * 3 + b] = im
            rows = pl.ds(i * BLOCK, BLOCK)
            zero = jnp.zeros((8, LANES), jnp.float32)
            products[rows, pl.ds(column, LANES)] = jnp.concatenate(
                re_tiles + [zero], axis=0
            ).astype(jnp.bfloat16)
            products[rows, pl.ds(column + LANES, LANES)] = jnp.concatenate(
                im_tiles + [zero], axis=0
            ).astype(jnp.bfloat16)
            return carry

        lax.fori_loop(0, FC, chunk, 0)
        count = None
        for w in range(WIN):
            g = s_tile(w) * t_tile(w)
            count = g if count is None else count + g
        for half in range(2):
            totals[pl.ds(half * 4 * BLOCK + order[i] * BLOCK + 72, 8), :] = count

    def transform(low, high):
        term = jnp.dot(
            products[low * BLOCK : high * BLOCK, :], table[...], preferred_element_type=jnp.float32
        ) * (1.0 / math.sqrt(BINS))
        for i in range(low, high):
            for half in range(2):
                rows = pl.ds(pl.multiple_of(half * 4 * BLOCK + order[i] * BLOCK, 8), 72)
                totals[rows, :] = term[
                    (i - low) * BLOCK : (i - low) * BLOCK + 72, half * LANES : (half + 1) * LANES
                ]

    arrive(1)
    for step in (1, 3, 2):
        x_copy(step, (x0 - step + 4) % 4).wait_recv()
    for slot in range(4):
        values = s_blocks[slot].astype(jnp.float32)
        s_wide[slot * ROWS : (slot + 1) * ROWS, :] = values
        s_wide[(4 + slot) * ROWS : (5 + slot) * ROWS, :] = values
    core_copy(0, 1 - c0).wait_recv()
    cross(0)
    arrive(2)
    core_copy(1, 1 - c0).wait_recv()
    cross(1)
    arrive(3)
    core_copy(2, 1 - c0).wait_recv()
    cross(2)
    table_copy.wait()
    transform(0, 3)
    core_copy(3, 1 - c0).wait_recv()
    cross(3)
    transform(3, 4)

    def hour_copy(step, slot):
        return pltpu.make_async_remote_copy(
            src_ref=result.at[step],
            dst_ref=hour_recv.at[slot],
            send_sem=hs.at[step],
            recv_sem=hr.at[step],
            device_id=at((x0 + step) % 4, z0, c0, day),
            device_id_type=MESH,
        )

    def ref_copy(step, h, slot):
        return pltpu.make_async_remote_copy(
            src_ref=result.at[step, h],
            dst_ref=ref_recv.at[slot],
            send_sem=rs.at[step, h],
            recv_sem=rr.at[slot],
            device_id=at((x0 + step) % 4, z0, c0, x0 * 2 + h),
            device_id_type=MESH,
        )

    for h in range(2):
        for step in (2, 1, 3, 0):
            x = (x0 + step) % 4
            starts = [
                half * 4 * BLOCK + (2 * h + bit) * BLOCK + core * 4 + x
                for bit in range(2)
                for core in range(2)
                for half in range(2)
            ]
            tiles = [totals[pl.ds(first, 8, stride=8), :] for first in starts]
            rest = [totals[pl.ds(first + 64, 2, stride=8), :] for first in starts]
            result[step, h] = jnp.concatenate(tiles + rest, axis=0).astype(jnp.bfloat16)
            if h == 0:

                @pl.when(jnp.logical_not(early))
                def _():
                    ref_copy(step, 0, day).start()

    def send_ref(step, h):
        if step:
            ref_copy(step, h, day).start()
        else:
            local = jnp.logical_and(mine, h0 == h)

            @pl.when(local)
            def _():
                ref_recv[day] = result[0, h]

            @pl.when(jnp.logical_not(local))
            def _():
                ref_copy(0, h, day).start()

    @pl.when(early)
    def _():
        for step in (2, 1, 3, 0):
            send_ref(step, 0)

    @pl.when(jnp.logical_not(early))
    def _():
        for step in (2, 1, 3, 0):
            send_ref(step, 1)

    for step in (2, 1, 3):
        hour_copy(step, x0).start()
    hour_recv[x0] = result[0]

    @pl.when(early)
    def _():
        pl.semaphore_wait(ready, 4)
        for step in (2, 1, 3, 0):
            ref_copy(step, 1, day).start()

    for step in (1, 3, 2):
        hour_copy(step, (x0 - step + 4) % 4).wait_recv()
    for x in range(4):
        for h in range(2):
            got = hour_recv[x, h].astype(jnp.float32)
            hour_wide[x * 128 + h * 64 : x * 128 + h * 64 + 64, :] = got[0:64]
            hour_rest[x * 32 + h * 16 : x * 32 + h * 16 + 16, :] = got[64:80]

    def hour_tile(x, half, p):
        if p < 8:
            return hour_wide[pl.ds(x * 128 + half * 8 + p, 8, stride=16), :]
        return hour_rest[pl.ds(x * 32 + half * 2 + p - 8, 8, stride=4), :]

    for pair in range(2):
        for half in range(2):
            factors = [
                mask_col[x * 8 : x * 8 + 8, :] / jnp.maximum(hour_tile(x, half, 9), 1.0)
                for x in (pair * 2, pair * 2 + 1)
            ]
            for p in range(9):
                tiles = [hour_tile(pair * 2 + i, half, p) * factors[i] for i in range(2)]
                hourly_ref[
                    0, p, 0, pair * 16 : pair * 16 + 16, half * LANES : (half + 1) * LANES
                ] = jnp.concatenate(tiles, axis=0).astype(jnp.bfloat16)

    for d in range(8):

        @pl.when(jnp.logical_not(jnp.logical_and(mine, day == d)))
        def _():
            ref_copy(1, 0, d).wait_recv()

    summed = ref_recv[0].astype(jnp.float32)
    for d in range(1, 8):
        summed = summed + ref_recv[d].astype(jnp.float32)
    ref_wide[...] = summed

    def share(half, p):
        if p < 8:
            return ref_wide[pl.ds(half * 8 + p, 4, stride=16), :]
        return ref_wide[pl.ds(64 + half * 2 + p - 8, 4, stride=4), :]

    for half in range(2):
        factor = mask_own[0:4, :] / jnp.maximum(share(half, 9), 1.0)
        for p in range(9):
            stack_ref[p, 0, :, half * LANES : (half + 1) * LANES] = share(half, p) * factor

    for step in (1, 3):
        z_copy(step, own).wait_send()

    @pl.when(outer)
    def _():
        z_copy(2, own).wait_send()

    @pl.when(inner)
    def _():
        relay(own, z0).wait_send()

    for step in (1, 2, 3):
        x_copy(step, x0).wait_send()
        hour_copy(step, x0).wait_send()
        for h in range(2):
            ref_copy(step, h, day).wait_send()
    for i in range(4):
        core_copy(i, c0).wait_send()
    for h in range(2):

        @pl.when(jnp.logical_not(jnp.logical_and(mine, h0 == h)))
        def _():
            ref_copy(0, h, day).wait_send()


def on_device(spectra, flags, pair_mask):
    table = jnp.asarray(lag_table())
    bf16, f32 = jnp.bfloat16, jnp.float32
    dma = pltpu.SemaphoreType.DMA
    vmem = pltpu.VMEM
    operands = (jnp.transpose(spectra, (0, 1, 3, 2, 4)), flags, pair_mask, table)
    return pl.pallas_call(
        kernel,
        out_shape=(
            jax.ShapeDtypeStruct((1, 9, 1, 32, LAGS), bf16),
            jax.ShapeDtypeStruct((9, 1, 4, LAGS), f32),
        ),
        in_specs=[pl.BlockSpec(memory_space=pl.ANY)] * 4,
        out_specs=(
            pl.BlockSpec(memory_space=pltpu.VMEM),
            pl.BlockSpec(memory_space=pltpu.VMEM),
        ),
        scratch_shapes=[
            vmem((1, 2, 3, WIN, BINS), bf16),
            vmem((1, WIN), jnp.int32),
            vmem((1, 32), jnp.int32),
            vmem((8, BINS + PAD), f32),
            vmem((ROWS, LANES), f32),
            vmem((8, ROWS, LANES), bf16),
            vmem((4, ROWS, LANES), bf16),
            vmem((2 * ROWS, LANES), f32),
            vmem((8 * ROWS, LANES), f32),
            vmem((2 * BINS, LAGS), bf16),
            vmem((4 * BLOCK, 2 * BINS), bf16),
            vmem((8 * BLOCK, LANES), f32),
            vmem((32, LANES), f32),
            vmem((8, LANES), f32),
            vmem((4, 2, BLOCK, LANES), bf16),
            vmem((4, 2, BLOCK, LANES), bf16),
            vmem((8, BLOCK, LANES), bf16),
            vmem((4 * 128, LANES), f32),
            vmem((4 * 32, LANES), f32),
            vmem((BLOCK, LANES), f32),
            dma((3,)),
            dma,
            dma((4,)),
            dma((4,)),
            dma,
            dma((4,)),
            dma((4,)),
            dma((4,)),
            dma((4,)),
            dma((4,)),
            dma((4,)),
            dma((4, 2)),
            dma((8,)),
            pltpu.SemaphoreType.REGULAR,
        ],
        compiler_params=pltpu.CompilerParams(
            collective_id=0, has_side_effects=True, vmem_limit_bytes=32 * 1024 * 1024
        ),
        cost_estimate=pl.CostEstimate(
            flops=500_000_000, bytes_accessed=2_000_000, transcendentals=6144
        ),
    )(*(pltpu.with_memory_space_constraint(a, pltpu.HBM) for a in operands))


def solution(mesh):
    placed = (P("sta", None, "day", None, None), P("sta", "day"), P("sta", None))
    return jax.shard_map(
        on_device,
        mesh=mesh,
        in_specs=placed,
        out_specs=(P("day", None, "sta", None, None), P(None, "sta", "day", None)),
        check_vma=False,
    )
```

```python
import math

import jax
import jax.numpy as jnp
import ml_dtypes
import numpy as np
from jax import lax
from jax.experimental import pallas as pl
from jax.experimental.pallas import tpu as pltpu
from jax.sharding import PartitionSpec as P

BINS = 1536
LAGS = 256
HALF_BAND = 16
WIN = 4
LANES = 128
FC = BINS // LANES
ROWS_FC = 24
FLAG_ROWS = 16
ROWS = FLAG_ROWS + FC * ROWS_FC
BLOCK = 80
PAD = 128
MESH = pl.DeviceIdType.MESH


def lag_table():
    freq = np.arange(BINS, dtype=np.int64)
    lag = np.arange(LAGS, dtype=np.int64) - LAGS // 2
    angle = (freq[:, None] * lag[None, :] % (2 * BINS)) * (math.pi / BINS)
    parts = np.stack([np.cos(angle), -np.sin(angle)]).reshape(2, FC, LANES, LAGS)
    rows = np.transpose(parts, (1, 0, 2, 3)).reshape(2 * BINS, LAGS)
    return rows.astype(np.float32).astype(ml_dtypes.bfloat16)


def kernel(
    spec_hbm, flags_hbm, mask_hbm, table_hbm,
    hourly_ref, stack_ref,
    spec_ref, flags_ref, mask_ref, power, white, t_blocks, s_blocks, t_wide, s_wide, s_tiles, table, products, totals,
    mask_col, mask_own, result, hour_recv, ref_recv, hour_wide, hour_rest, ref_wide,
    in_sems, table_sem, zs, zr, fs, xs, xr, cs, cr, hs, hr, rs, rr, ready,
):
    sta = lax.axis_index("sta")
    day = lax.axis_index("day")
    x0, z0, c0 = sta // 8, (sta // 2) % 4, sta % 2
    y0, h0 = day // 2, day % 2

    def sta_of(x, z, c):
        return (x * 4 + z) * 2 + c

    def at(x, z, c, d):
        return (sta_of(x, z, c), d)

    sibling = at(x0, z0, 1 - c0, day)

    barrier = pltpu.get_barrier_semaphore()

    def greet(target):
        pl.semaphore_signal(barrier, inc=1, device_id=target, device_id_type=MESH)

    for step in (3, 1, 2):
        greet(at(x0, (z0 + step) % 4, c0, day))
    for step in (2, 1, 3):
        greet(at((x0 + step) % 4, z0, c0, day))
    greet(sibling)
    mine = x0 == y0
    early = h0 == 0
    for y in range(4):

        @pl.when(y != y0)
        def _():
            greet(at(x0, z0, c0, y * 2 + h0))

        @pl.when(early)
        def _():
            greet(at(y0, z0, c0, y * 2 + 1))
            greet(at(y, z0, c0, x0 * 2 + 1))

    loads = [
        pltpu.make_async_copy(spec_hbm, spec_ref, in_sems.at[0]),
        pltpu.make_async_copy(flags_hbm, flags_ref, in_sems.at[1]),
        pltpu.make_async_copy(mask_hbm, mask_ref, in_sems.at[2]),
    ]
    for load in loads:
        load.start()
    table_copy = pltpu.make_async_copy(table_hbm, table, table_sem)
    table_copy.start()

    loads[0].wait()
    loads[1].wait()
    power[...] = jnp.zeros_like(power)
    energy = None
    for part in range(2):
        for comp in range(3):
            values = spec_ref[0, part, comp].astype(jnp.float32)
            energy = values * values if energy is None else energy + values * values
    power[0:WIN, 0:BINS] = energy
    single = power[...]
    span = single
    for shift in (1, 2, 4, 8, 16):
        span = span + pltpu.roll(span, shift, axis=1)
    span = span + pltpu.roll(single, 2 * HALF_BAND, axis=1)
    smooth = pltpu.roll(span, BINS + PAD - HALF_BAND, axis=1)[0:WIN, 0:BINS]
    line = lax.broadcasted_iota(jnp.int32, (WIN, WIN), 0)
    place = lax.broadcasted_iota(jnp.int32, (WIN, WIN), 1)
    spread = jnp.broadcast_to((1 - flags_ref[...]).astype(jnp.float32), (WIN, WIN))
    good = jnp.sum(jnp.where(line == place, spread, 0.0), axis=1, keepdims=True)
    scale = lax.rsqrt(smooth / (6.0 * (2 * HALF_BAND + 1)) + 1e-06) * good
    for part in range(2):
        for comp in range(3):
            y = spec_ref[0, part, comp].astype(jnp.float32) * scale
            first = FLAG_ROWS + (part * 3 + comp) * WIN
            for fc in range(FC):
                white[first + fc * ROWS_FC : first + fc * ROWS_FC + WIN, :] = y[
                    :, fc * LANES : (fc + 1) * LANES
                ]
    white[0:WIN, :] = jnp.broadcast_to(good, (WIN, LANES))
    white[WIN:FLAG_ROWS, :] = jnp.zeros((FLAG_ROWS - WIN, LANES), jnp.float32)
    block = white[...].astype(jnp.bfloat16)
    own = z0 * 2 + c0
    t_blocks[own] = block
    s_blocks[x0] = block

    loads[2].wait()
    spread = jnp.broadcast_to(mask_ref[...].astype(jnp.float32), (32, 32))
    line = lax.broadcasted_iota(jnp.int32, (32, 32), 0)
    place = lax.broadcasted_iota(jnp.int32, (32, 32), 1)
    column = jnp.sum(jnp.where(line == place, spread, 0.0), axis=1, keepdims=True)
    mask_col[...] = jnp.broadcast_to(column, (32, LANES))
    column = jnp.sum(
        jnp.where(line[0:8] + day * 4 == place[0:8], spread[0:8], 0.0), axis=1, keepdims=True
    )
    mask_own[...] = jnp.broadcast_to(column, (8, LANES))

    @pl.when(early)
    def _():
        pl.semaphore_wait(barrier, 10)

    @pl.when(jnp.logical_not(early))
    def _():
        pl.semaphore_wait(barrier, 18)
        for y in range(4):
            pl.semaphore_signal(
                ready, inc=1, device_id=at(y0, z0, c0, y * 2), device_id_type=MESH
            )


    def z_copy(step, slot):
        return pltpu.make_async_remote_copy(
            src_ref=t_blocks.at[own],
            dst_ref=t_blocks.at[slot],
            send_sem=zs.at[step],
            recv_sem=zr.at[step],
            device_id=at(x0, (z0 + step) % 4, c0, day),
            device_id_type=MESH,
        )

    def relay(slot, z):
        return pltpu.make_async_remote_copy(
            src_ref=t_blocks.at[slot],
            dst_ref=t_blocks.at[slot],
            send_sem=fs,
            recv_sem=zr.at[2],
            device_id=at(x0, z, c0, day),
            device_id_type=MESH,
        )

    def x_copy(step, slot):
        return pltpu.make_async_remote_copy(
            src_ref=s_blocks.at[x0],
            dst_ref=s_blocks.at[slot],
            send_sem=xs.at[step],
            recv_sem=xr.at[step],
            device_id=at((x0 + step) % 4, z0, c0, day),
            device_id_type=MESH,
        )

    order = [z0, z0 + 1 - 2 * (z0 % 2), 3 - z0, (z0 + 2) % 4]

    def core_copy(i, core):
        slot = order[i] * 2 + core
        return pltpu.make_async_remote_copy(
            src_ref=t_blocks.at[slot],
            dst_ref=t_blocks.at[slot],
            send_sem=cs.at[i],
            recv_sem=cr.at[i],
            device_id=sibling,
            device_id_type=MESH,
        )

    outer = jnp.logical_or(z0 == 0, z0 == 3)
    inner = jnp.logical_not(outer)

    @pl.when(z0 % 2 == 0)
    def _():
        z_copy(1, own).start()
        z_copy(3, own).start()

    @pl.when(z0 % 2 == 1)
    def _():
        z_copy(3, own).start()
        z_copy(1, own).start()

    for step in (2, 1, 3):
        x_copy(step, x0).start()

    @pl.when(outer)
    def _():
        z_copy(2, own).start()

    core_copy(0, c0).start()

    def arrive(i):
        slot = order[i] * 2 + c0
        z_copy((z0 - order[i] + 4) % 4, slot).wait_recv()
        core_copy(i, c0).start()

    high_rows = lax.broadcasted_iota(jnp.int32, (8, LANES), 0) >= 4

    def t_tile(row):
        first = jnp.broadcast_to(t_wide[pl.ds(row, 1), :], (8, LANES))
        second = jnp.broadcast_to(t_wide[pl.ds(ROWS + row, 1), :], (8, LANES))
        return jnp.where(high_rows, second, first)

    def s_tile(row):
        return s_tiles[pl.ds(pl.multiple_of(row * 8, 8), 8), :]

    def cross(i):
        for core in range(2):
            t_wide[core * ROWS : (core + 1) * ROWS, :] = t_blocks[order[i] * 2 + core].astype(
                jnp.float32
            )

        def chunk(fc, carry):
            base = FLAG_ROWS + fc * ROWS_FC
            local = [s_tile(base + r) for r in range(ROWS_FC)]
            column = pl.multiple_of(fc * 2 * LANES, 2 * LANES)
            re_tiles, im_tiles = [None] * 9, [None] * 9
            for b in range(3):
                other = [
                    t_tile(base + (part * 3 + b) * WIN + w) for part in range(2) for w in range(WIN)
                ]
                for a in range(3):
                    re, im = None, None
                    for w in range(WIN):
                        s_re, s_im = local[a * WIN + w], local[(3 + a) * WIN + w]
                        t_re, t_im = other[w], other[WIN + w]
                        re_term = s_re * t_re + s_im * t_im
                        im_term = s_im * t_re - s_re * t_im
                        re = re_term if re is None else re + re_term
                        im = im_term if im is None else im + im_term
                    re_tiles[a * 3 + b] = re
                    im_tiles[a * 3 + b] = im
            rows = pl.ds(i * BLOCK, BLOCK)
            zero = jnp.zeros((8, LANES), jnp.float32)
            products[rows, pl.ds(column, LANES)] = jnp.concatenate(
                re_tiles + [zero], axis=0
            ).astype(jnp.bfloat16)
            products[rows, pl.ds(column + LANES, LANES)] = jnp.concatenate(
                im_tiles + [zero], axis=0
            ).astype(jnp.bfloat16)
            return carry

        lax.fori_loop(0, FC, chunk, 0)
        count = None
        for w in range(WIN):
            g = s_tile(w) * t_tile(w)
            count = g if count is None else count + g
        for half in range(2):
            totals[pl.ds(half * 4 * BLOCK + order[i] * BLOCK + 72, 8), :] = count

    def transform(low, high):
        term = jnp.dot(
            products[low * BLOCK : high * BLOCK, :], table[...], preferred_element_type=jnp.float32
        ) * (1.0 / math.sqrt(BINS))
        for i in range(low, high):
            for half in range(2):
                rows = pl.ds(pl.multiple_of(half * 4 * BLOCK + order[i] * BLOCK, 8), 72)
                totals[rows, :] = term[
                    (i - low) * BLOCK : (i - low) * BLOCK + 72, half * LANES : (half + 1) * LANES
                ]

    def hour_copy(step, slot):
        return pltpu.make_async_remote_copy(
            src_ref=result.at[step],
            dst_ref=hour_recv.at[slot],
            send_sem=hs.at[step],
            recv_sem=hr.at[step],
            device_id=at((x0 + step) % 4, z0, c0, day),
            device_id_type=MESH,
        )

    def ref_copy(step, h, slot):
        return pltpu.make_async_remote_copy(
            src_ref=result.at[step, h],
            dst_ref=ref_recv.at[slot],
            send_sem=rs.at[step, h],
            recv_sem=rr.at[slot],
            device_id=at((x0 + step) % 4, z0, c0, x0 * 2 + h),
            device_id_type=MESH,
        )

    def send_share(h):
        for step in (2, 1, 3, 0):
            x = (x0 + step) % 4
            starts = [
                half * 4 * BLOCK + (2 * h + bit) * BLOCK + core * 4 + x
                for bit in range(2)
                for core in range(2)
                for half in range(2)
            ]
            tiles = [totals[pl.ds(first, 8, stride=8), :] for first in starts]
            rest = [totals[pl.ds(first + 64, 2, stride=8), :] for first in starts]
            result[step, h] = jnp.concatenate(tiles + rest, axis=0).astype(jnp.bfloat16)
            now = jnp.logical_or(jnp.logical_not(early), h == 0)
            if step == 0:
                local = jnp.logical_and(mine, h0 == h)

                @pl.when(local)
                def _():
                    ref_recv[day] = result[0, h]

                now = jnp.logical_and(now, jnp.logical_not(local))

            @pl.when(now)
            def _():
                ref_copy(step, h, day).start()

    arrive(1)

    @pl.when(inner)
    def _():
        arrive(2)
        relay(order[2] * 2 + c0, 3 * (z0 - 1)).start()

    for step in (1, 3, 2):
        x_copy(step, (x0 - step + 4) % 4).wait_recv()
    for slot in range(4):
        values = s_blocks[slot].astype(jnp.float32)
        s_wide[slot * ROWS : (slot + 1) * ROWS, :] = values
        s_wide[(4 + slot) * ROWS : (5 + slot) * ROWS, :] = values

    def prepare(i, carry):
        for r in range(16):
            row = i * 16 + r
            s_tiles[pl.ds(pl.multiple_of(row * 8, 8), 8), :] = s_wide[
                pl.ds(row, 8, stride=ROWS), :
            ]
        return carry

    lax.fori_loop(0, ROWS // 16, prepare, 0)
    core_copy(0, 1 - c0).wait_recv()
    cross(0)
    core_copy(1, 1 - c0).wait_recv()
    cross(1)
    table_copy.wait()

    @pl.when(z0 < 2)
    def _():
        transform(0, 2)
        send_share(z0 // 2)

    @pl.when(outer)
    def _():
        arrive(2)

    core_copy(2, 1 - c0).wait_recv()
    cross(2)
    arrive(3)
    core_copy(3, 1 - c0).wait_recv()
    cross(3)
    transform(2, 4)
    send_share(1 - z0 // 2)

    @pl.when(z0 >= 2)
    def _():
        transform(0, 2)
        send_share(z0 // 2)

    for step in (2, 1, 3):
        hour_copy(step, x0).start()
    hour_recv[x0] = result[0]

    @pl.when(early)
    def _():
        pl.semaphore_wait(ready, 4)
        for step in (2, 1, 3, 0):
            ref_copy(step, 1, day).start()

    for step in (1, 3, 2):
        hour_copy(step, (x0 - step + 4) % 4).wait_recv()
    for x in range(4):
        for h in range(2):
            got = hour_recv[x, h].astype(jnp.float32)
            hour_wide[x * 128 + h * 64 : x * 128 + h * 64 + 64, :] = got[0:64]
            hour_rest[x * 32 + h * 16 : x * 32 + h * 16 + 16, :] = got[64:80]

    def hour_tile(x, half, p):
        if p < 8:
            return hour_wide[pl.ds(x * 128 + half * 8 + p, 8, stride=16), :]
        return hour_rest[pl.ds(x * 32 + half * 2 + p - 8, 8, stride=4), :]

    for pair in range(2):
        for half in range(2):
            factors = [
                mask_col[x * 8 : x * 8 + 8, :] / jnp.maximum(hour_tile(x, half, 9), 1.0)
                for x in (pair * 2, pair * 2 + 1)
            ]
            for p in range(9):
                tiles = [hour_tile(pair * 2 + i, half, p) * factors[i] for i in range(2)]
                hourly_ref[
                    0, p, 0, pair * 16 : pair * 16 + 16, half * LANES : (half + 1) * LANES
                ] = jnp.concatenate(tiles, axis=0).astype(jnp.bfloat16)

    for d in range(8):

        @pl.when(jnp.logical_not(jnp.logical_and(mine, day == d)))
        def _():
            ref_copy(1, 0, d).wait_recv()

    summed = ref_recv[0].astype(jnp.float32)
    for d in range(1, 8):
        summed = summed + ref_recv[d].astype(jnp.float32)
    ref_wide[...] = summed

    def share(half, p):
        if p < 8:
            return ref_wide[pl.ds(half * 8 + p, 4, stride=16), :]
        return ref_wide[pl.ds(64 + half * 2 + p - 8, 4, stride=4), :]

    for half in range(2):
        factor = mask_own[0:4, :] / jnp.maximum(share(half, 9), 1.0)
        for p in range(9):
            stack_ref[p, 0, :, half * LANES : (half + 1) * LANES] = share(half, p) * factor

    for step in (1, 3):
        z_copy(step, own).wait_send()

    @pl.when(outer)
    def _():
        z_copy(2, own).wait_send()

    @pl.when(inner)
    def _():
        relay(own, z0).wait_send()

    for step in (1, 2, 3):
        x_copy(step, x0).wait_send()
        hour_copy(step, x0).wait_send()
        for h in range(2):
            ref_copy(step, h, day).wait_send()
    for i in range(4):
        core_copy(i, c0).wait_send()
    for h in range(2):

        @pl.when(jnp.logical_not(jnp.logical_and(mine, h0 == h)))
        def _():
            ref_copy(0, h, day).wait_send()


def write_out(hourly_ref, stack_ref, hourly_hbm, stack_hbm, sems):
    copies = [
        pltpu.make_async_copy(hourly_ref, hourly_hbm, sems.at[0]),
        pltpu.make_async_copy(stack_ref, stack_hbm, sems.at[1]),
    ]
    for copy in copies:
        copy.start()
    for copy in copies:
        copy.wait()


def on_device(spectra, flags, pair_mask):
    table = jnp.asarray(lag_table())
    bf16, f32 = jnp.bfloat16, jnp.float32
    dma = pltpu.SemaphoreType.DMA
    vmem = pltpu.VMEM
    operands = (jnp.transpose(spectra, (0, 1, 3, 2, 4)), flags, pair_mask, table)
    shapes = (
        jax.ShapeDtypeStruct((1, 9, 1, 32, LAGS), bf16),
        jax.ShapeDtypeStruct((9, 1, 4, LAGS), f32),
    )
    results = pl.pallas_call(
        kernel,
        out_shape=shapes,
        in_specs=[pl.BlockSpec(memory_space=pl.ANY)] * 4,
        out_specs=(
            pl.BlockSpec(memory_space=pltpu.VMEM),
            pl.BlockSpec(memory_space=pltpu.VMEM),
        ),
        scratch_shapes=[
            vmem((1, 2, 3, WIN, BINS), bf16),
            vmem((1, WIN), jnp.int32),
            vmem((1, 32), jnp.int32),
            vmem((8, BINS + PAD), f32),
            vmem((ROWS, LANES), f32),
            vmem((8, ROWS, LANES), bf16),
            vmem((4, ROWS, LANES), bf16),
            vmem((2 * ROWS, LANES), f32),
            vmem((8 * ROWS, LANES), f32),
            vmem((8 * ROWS, LANES), f32),
            vmem((2 * BINS, LAGS), bf16),
            vmem((4 * BLOCK, 2 * BINS), bf16),
            vmem((8 * BLOCK, LANES), f32),
            vmem((32, LANES), f32),
            vmem((8, LANES), f32),
            vmem((4, 2, BLOCK, LANES), bf16),
            vmem((4, 2, BLOCK, LANES), bf16),
            vmem((8, BLOCK, LANES), bf16),
            vmem((4 * 128, LANES), f32),
            vmem((4 * 32, LANES), f32),
            vmem((BLOCK, LANES), f32),
            dma((3,)),
            dma,
            dma((4,)),
            dma((4,)),
            dma,
            dma((4,)),
            dma((4,)),
            dma((4,)),
            dma((4,)),
            dma((4,)),
            dma((4,)),
            dma((4, 2)),
            dma((8,)),
            pltpu.SemaphoreType.REGULAR,
        ],
        compiler_params=pltpu.CompilerParams(
            collective_id=0, has_side_effects=True, vmem_limit_bytes=32 * 1024 * 1024
        ),
        cost_estimate=pl.CostEstimate(
            flops=500_000_000, bytes_accessed=2_000_000, transcendentals=6144
        ),
    )(*(pltpu.with_memory_space_constraint(a, pltpu.HBM) for a in operands))
    return pl.pallas_call(
        write_out,
        out_shape=shapes,
        in_specs=[pl.BlockSpec(memory_space=pltpu.VMEM)] * 2,
        out_specs=(pl.BlockSpec(memory_space=pl.ANY),) * 2,
        scratch_shapes=[dma((2,))],
        compiler_params=pltpu.CompilerParams(vmem_limit_bytes=1024 * 1024),
    )(*results)


def solution(mesh):
    placed = (P("sta", None, "day", None, None), P("sta", "day"), P("sta", None))
    return jax.shard_map(
        on_device,
        mesh=mesh,
        in_specs=placed,
        out_specs=(P("day", None, "sta", None, None), P(None, "sta", "day", None)),
        check_vma=False,
    )
```

```python
import math

import jax
import jax.numpy as jnp
import ml_dtypes
import numpy as np
from jax import lax
from jax.experimental import pallas as pl
from jax.experimental.pallas import tpu as pltpu
from jax.sharding import PartitionSpec as P

BINS = 1536
LAGS = 256
HALF_BAND = 16
WIN = 4
LANES = 128
FC = BINS // LANES
ROWS_FC = 24
FLAG_ROWS = 16
ROWS = FLAG_ROWS + FC * ROWS_FC
BLOCK = 80
PAD = 128
MESH = pl.DeviceIdType.MESH


def lag_table():
    freq = np.arange(BINS, dtype=np.int64)
    lag = np.arange(LAGS, dtype=np.int64) - LAGS // 2
    angle = (freq[:, None] * lag[None, :] % (2 * BINS)) * (math.pi / BINS)
    parts = np.stack([np.cos(angle), -np.sin(angle)]).reshape(2, FC, LANES, LAGS)
    rows = np.transpose(parts, (1, 0, 2, 3)).reshape(2 * BINS, LAGS)
    return rows.astype(np.float32).astype(ml_dtypes.bfloat16)


def kernel(
    spec_hbm, flags_hbm, mask_hbm, table_hbm,
    hourly_ref, stack_ref,
    spec_ref, flags_ref, mask_ref, power, white, t_blocks, s_blocks, t_wide, s_wide, s_tiles, table, products, totals,
    mask_col, mask_own, result, hour_recv, ref_recv, hour_wide, hour_rest, ref_wide,
    in_sems, table_sem, zs, zr, fs, xs, xr, cs, cr, hs, hr, rs, rr, ready,
):
    sta = lax.axis_index("sta")
    day = lax.axis_index("day")
    x0, z0, c0 = sta // 8, (sta // 2) % 4, sta % 2
    y0, h0 = day // 2, day % 2

    def sta_of(x, z, c):
        return (x * 4 + z) * 2 + c

    def at(x, z, c, d):
        return (sta_of(x, z, c), d)

    sibling = at(x0, z0, 1 - c0, day)

    barrier = pltpu.get_barrier_semaphore()

    def greet(target):
        pl.semaphore_signal(barrier, inc=1, device_id=target, device_id_type=MESH)

    for step in (3, 1, 2):
        greet(at(x0, (z0 + step) % 4, c0, day))
    for step in (2, 1, 3):
        greet(at((x0 + step) % 4, z0, c0, day))
    greet(sibling)
    mine = x0 == y0
    early = h0 == 0
    for y in range(4):

        @pl.when(y != y0)
        def _():
            greet(at(x0, z0, c0, y * 2 + h0))

        @pl.when(early)
        def _():
            greet(at(y0, z0, c0, y * 2 + 1))
            greet(at(y, z0, c0, x0 * 2 + 1))

    loads = [
        pltpu.make_async_copy(spec_hbm, spec_ref, in_sems.at[0]),
        pltpu.make_async_copy(flags_hbm, flags_ref, in_sems.at[1]),
        pltpu.make_async_copy(mask_hbm, mask_ref, in_sems.at[2]),
    ]
    for load in loads:
        load.start()
    table_copy = pltpu.make_async_copy(table_hbm, table, table_sem)
    table_copy.start()

    loads[0].wait()
    loads[1].wait()
    power[...] = jnp.zeros_like(power)
    energy = None
    for part in range(2):
        for comp in range(3):
            values = spec_ref[0, part, comp].astype(jnp.float32)
            energy = values * values if energy is None else energy + values * values
    power[0:WIN, 0:BINS] = energy
    single = power[...]
    span = single
    for shift in (1, 2, 4, 8, 16):
        span = span + pltpu.roll(span, shift, axis=1)
    span = span + pltpu.roll(single, 2 * HALF_BAND, axis=1)
    smooth = pltpu.roll(span, BINS + PAD - HALF_BAND, axis=1)[0:WIN, 0:BINS]
    line = lax.broadcasted_iota(jnp.int32, (WIN, WIN), 0)
    place = lax.broadcasted_iota(jnp.int32, (WIN, WIN), 1)
    spread = jnp.broadcast_to((1 - flags_ref[...]).astype(jnp.float32), (WIN, WIN))
    good = jnp.sum(jnp.where(line == place, spread, 0.0), axis=1, keepdims=True)
    scale = lax.rsqrt(smooth / (6.0 * (2 * HALF_BAND + 1)) + 1e-06) * good
    for part in range(2):
        for comp in range(3):
            y = spec_ref[0, part, comp].astype(jnp.float32) * scale
            first = FLAG_ROWS + (part * 3 + comp) * WIN
            for fc in range(FC):
                white[first + fc * ROWS_FC : first + fc * ROWS_FC + WIN, :] = y[
                    :, fc * LANES : (fc + 1) * LANES
                ]
    white[0:WIN, :] = jnp.broadcast_to(good, (WIN, LANES))
    white[WIN:FLAG_ROWS, :] = jnp.zeros((FLAG_ROWS - WIN, LANES), jnp.float32)
    block = white[...].astype(jnp.bfloat16)
    own = z0 * 2 + c0
    t_blocks[own] = block
    s_blocks[x0] = block

    loads[2].wait()
    spread = jnp.broadcast_to(mask_ref[...].astype(jnp.float32), (32, 32))
    line = lax.broadcasted_iota(jnp.int32, (32, 32), 0)
    place = lax.broadcasted_iota(jnp.int32, (32, 32), 1)
    column = jnp.sum(jnp.where(line == place, spread, 0.0), axis=1, keepdims=True)
    mask_col[...] = jnp.broadcast_to(column, (32, LANES))
    column = jnp.sum(
        jnp.where(line[0:8] + day * 4 == place[0:8], spread[0:8], 0.0), axis=1, keepdims=True
    )
    mask_own[...] = jnp.broadcast_to(column, (8, LANES))

    @pl.when(early)
    def _():
        pl.semaphore_wait(barrier, 10)

    @pl.when(jnp.logical_not(early))
    def _():
        pl.semaphore_wait(barrier, 18)
        for y in range(4):
            pl.semaphore_signal(
                ready, inc=1, device_id=at(y0, z0, c0, y * 2), device_id_type=MESH
            )


    def z_copy(step, slot):
        return pltpu.make_async_remote_copy(
            src_ref=t_blocks.at[own],
            dst_ref=t_blocks.at[slot],
            send_sem=zs.at[step],
            recv_sem=zr.at[step],
            device_id=at(x0, (z0 + step) % 4, c0, day),
            device_id_type=MESH,
        )

    def relay(slot, z):
        return pltpu.make_async_remote_copy(
            src_ref=t_blocks.at[slot],
            dst_ref=t_blocks.at[slot],
            send_sem=fs,
            recv_sem=zr.at[2],
            device_id=at(x0, z, c0, day),
            device_id_type=MESH,
        )

    def x_copy(step, slot):
        return pltpu.make_async_remote_copy(
            src_ref=s_blocks.at[x0],
            dst_ref=s_blocks.at[slot],
            send_sem=xs.at[step],
            recv_sem=xr.at[step],
            device_id=at((x0 + step) % 4, z0, c0, day),
            device_id_type=MESH,
        )

    outer = jnp.logical_or(z0 == 0, z0 == 3)
    inner = jnp.logical_not(outer)
    def core_copy(z, core):
        slot = z * 2 + core
        return pltpu.make_async_remote_copy(
            src_ref=t_blocks.at[slot],
            dst_ref=t_blocks.at[slot],
            send_sem=cs.at[z],
            recv_sem=cr.at[z],
            device_id=sibling,
            device_id_type=MESH,
        )

    @pl.when(z0 == 0)
    def _():
        z_copy(1, own).start()

    z_copy(3, own).start()

    @pl.when(z0 > 0)
    def _():
        z_copy(1, own).start()

    for step in (2, 1, 3):
        x_copy(step, x0).start()

    @pl.when(outer)
    def _():
        z_copy(2, own).start()

    core_copy(z0, c0).start()

    def arrive(z):
        z_copy((z0 - z + 4) % 4, z * 2 + c0).wait_recv()
        core_copy(z, c0).start()

    high_rows = lax.broadcasted_iota(jnp.int32, (8, LANES), 0) >= 4

    def t_tile(row):
        first = jnp.broadcast_to(t_wide[pl.ds(row, 1), :], (8, LANES))
        second = jnp.broadcast_to(t_wide[pl.ds(ROWS + row, 1), :], (8, LANES))
        return jnp.where(high_rows, second, first)

    def s_tile(row):
        return s_tiles[pl.ds(pl.multiple_of(row * 8, 8), 8), :]

    def cross(h, core):
        for bit in range(2):
            t_wide[bit * ROWS : (bit + 1) * ROWS, :] = t_blocks[(2 * h + bit) * 2 + core].astype(
                jnp.float32
            )

        def chunk(fc, carry):
            base = FLAG_ROWS + fc * ROWS_FC
            local = [s_tile(base + r) for r in range(ROWS_FC)]
            column = pl.multiple_of(fc * 2 * LANES, 2 * LANES)
            re_tiles, im_tiles = [None] * 9, [None] * 9
            for b in range(3):
                other = [
                    t_tile(base + (part * 3 + b) * WIN + w) for part in range(2) for w in range(WIN)
                ]
                for a in range(3):
                    re, im = None, None
                    for w in range(WIN):
                        s_re, s_im = local[a * WIN + w], local[(3 + a) * WIN + w]
                        t_re, t_im = other[w], other[WIN + w]
                        re_term = s_re * t_re + s_im * t_im
                        im_term = s_im * t_re - s_re * t_im
                        re = re_term if re is None else re + re_term
                        im = im_term if im is None else im + im_term
                    re_tiles[a * 3 + b] = re
                    im_tiles[a * 3 + b] = im
            rows = pl.ds(pl.multiple_of((2 * h + core) * BLOCK, 16), BLOCK)
            zero = jnp.zeros((8, LANES), jnp.float32)
            products[rows, pl.ds(column, LANES)] = jnp.concatenate(
                re_tiles + [zero], axis=0
            ).astype(jnp.bfloat16)
            products[rows, pl.ds(column + LANES, LANES)] = jnp.concatenate(
                im_tiles + [zero], axis=0
            ).astype(jnp.bfloat16)
            return carry

        lax.fori_loop(0, FC, chunk, 0)
        count = None
        for w in range(WIN):
            g = s_tile(w) * t_tile(w)
            count = g if count is None else count + g
        for half in range(2):
            first = (4 * half + 2 * h + core) * BLOCK + 72
            totals[pl.ds(pl.multiple_of(first, 8), 8), :] = count

    def transform(h, core):
        term = jnp.dot(
            products[pl.ds(pl.multiple_of((2 * h + core) * BLOCK, 16), BLOCK), :],
            table[...],
            preferred_element_type=jnp.float32,
        ) * (1.0 / math.sqrt(BINS))
        for half in range(2):
            first = pl.multiple_of((4 * half + 2 * h + core) * BLOCK, 8)
            totals[pl.ds(first, 72), :] = term[0:72, half * LANES : (half + 1) * LANES]

    def hour_copy(step, slot):
        return pltpu.make_async_remote_copy(
            src_ref=result.at[step],
            dst_ref=hour_recv.at[slot],
            send_sem=hs.at[step],
            recv_sem=hr.at[step],
            device_id=at((x0 + step) % 4, z0, c0, day),
            device_id_type=MESH,
        )

    def ref_copy(step, h, core, d):
        slot = core * 8 + d
        return pltpu.make_async_remote_copy(
            src_ref=result.at[step, core, h],
            dst_ref=ref_recv.at[slot],
            send_sem=rs.at[step, h, core],
            recv_sem=rr.at[slot],
            device_id=at((x0 + step) % 4, z0, c0, x0 * 2 + h),
            device_id_type=MESH,
        )

    def send_share(h, core):
        for step in (2, 1, 3, 0):
            x = (x0 + step) % 4
            starts = [
                (4 * half + 2 * h + core) * BLOCK + bit * 4 + x
                for bit in range(2)
                for half in range(2)
            ]
            tiles = [totals[pl.ds(first, 8, stride=8), :] for first in starts]
            rest = [totals[pl.ds(first + 64, 2, stride=8), :] for first in starts]
            zero = jnp.zeros((8, LANES), jnp.float32)
            result[step, core, h] = jnp.concatenate(tiles + rest + [zero], axis=0).astype(
                jnp.bfloat16
            )
            now = jnp.logical_or(jnp.logical_not(early), h == 0)
            if step == 0:
                local = jnp.logical_and(mine, h0 == h)

                @pl.when(local)
                def _():
                    ref_recv[core * 8 + day] = result[0, core, h]

                now = jnp.logical_and(now, jnp.logical_not(local))

            @pl.when(now)
            def _():
                ref_copy(step, h, core, day).start()

    @pl.when(outer)
    def _():
        arrive(1 + z0 // 3)

    @pl.when(z0 == 1)
    def _():
        arrive(0)

    @pl.when(inner)
    def _():
        arrive(3 - z0)
        relay((3 - z0) * 2 + c0, 3 * (z0 - 1)).start()

    for step in (1, 3, 2):
        x_copy(step, (x0 - step + 4) % 4).wait_recv()
    for slot in range(4):
        values = s_blocks[slot].astype(jnp.float32)
        s_wide[slot * ROWS : (slot + 1) * ROWS, :] = values
        s_wide[(4 + slot) * ROWS : (5 + slot) * ROWS, :] = values

    def prepare(i, carry):
        for r in range(16):
            row = i * 16 + r
            s_tiles[pl.ds(pl.multiple_of(row * 8, 8), 8), :] = s_wide[
                pl.ds(row, 8, stride=ROWS), :
            ]
        return carry

    lax.fori_loop(0, ROWS // 16, prepare, 0)
    def part(h, core):
        cross(h, core)
        transform(h, core)
        send_share(h, core)

    table_copy.wait()

    @pl.when(z0 == 3)
    def _():
        cross(1, c0)

    @pl.when(z0 >= 2)
    def _():
        arrive(0)

    @pl.when(z0 == 3)
    def _():
        arrive(1)

    part(0, c0)
    core_copy(0, 1 - c0).wait_recv()
    core_copy(1, 1 - c0).wait_recv()
    part(0, 1 - c0)

    @pl.when(z0 < 3)
    def _():
        arrive(3)

    @pl.when(z0 == 0)
    def _():
        arrive(2)

    @pl.when(z0 < 3)
    def _():
        cross(1, c0)

    core_copy(2, 1 - c0).wait_recv()
    core_copy(3, 1 - c0).wait_recv()
    transform(1, c0)
    send_share(1, c0)
    part(1, 1 - c0)

    for step in (2, 1, 3):
        hour_copy(step, x0).start()
    hour_recv[x0] = result[0]

    @pl.when(early)
    def _():
        pl.semaphore_wait(ready, 4)
        for step in (2, 1, 3, 0):
            for core in range(2):
                ref_copy(step, 1, core, day).start()

    for step in (1, 3, 2):
        hour_copy(step, (x0 - step + 4) % 4).wait_recv()
    for x in range(4):
        for core in range(2):
            for h in range(2):
                got = hour_recv[x, core, h].astype(jnp.float32)
                for bit in range(2):
                    for half in range(2):
                        tile = bit * 2 + half
                        t = (h * 2 + bit) * 2 + core
                        first = x * 128 + t * 16 + half * 8
                        hour_wide[first : first + 8, :] = got[tile * 8 : tile * 8 + 8]
                        first = x * 32 + t * 4 + half * 2
                        hour_rest[first : first + 2, :] = got[32 + tile * 2 : 34 + tile * 2]

    def hour_tile(x, half, p):
        if p < 8:
            return hour_wide[pl.ds(x * 128 + half * 8 + p, 8, stride=16), :]
        return hour_rest[pl.ds(x * 32 + half * 2 + p - 8, 8, stride=4), :]

    for pair in range(2):
        for half in range(2):
            factors = [
                mask_col[x * 8 : x * 8 + 8, :] / jnp.maximum(hour_tile(x, half, 9), 1.0)
                for x in (pair * 2, pair * 2 + 1)
            ]
            for p in range(9):
                tiles = [hour_tile(pair * 2 + i, half, p) * factors[i] for i in range(2)]
                hourly_ref[
                    0, p, 0, pair * 16 : pair * 16 + 16, half * LANES : (half + 1) * LANES
                ] = jnp.concatenate(tiles, axis=0).astype(jnp.bfloat16)

    for core in range(2):
        for d in range(8):

            @pl.when(jnp.logical_not(jnp.logical_and(mine, day == d)))
            def _():
                ref_copy(1, 0, core, d).wait_recv()

    for core in range(2):
        summed = ref_recv[core * 8].astype(jnp.float32)
        for d in range(1, 8):
            summed = summed + ref_recv[core * 8 + d].astype(jnp.float32)
        for bit in range(2):
            for half in range(2):
                tile = bit * 2 + half
                first = (bit * 2 + core) * 16 + half * 8
                ref_wide[first : first + 8, :] = summed[tile * 8 : tile * 8 + 8]
                first = 64 + (bit * 2 + core) * 4 + half * 2
                ref_wide[first : first + 2, :] = summed[32 + tile * 2 : 34 + tile * 2]

    def share(half, p):
        if p < 8:
            return ref_wide[pl.ds(half * 8 + p, 4, stride=16), :]
        return ref_wide[pl.ds(64 + half * 2 + p - 8, 4, stride=4), :]

    for half in range(2):
        factor = mask_own[0:4, :] / jnp.maximum(share(half, 9), 1.0)
        for p in range(9):
            stack_ref[p, 0, :, half * LANES : (half + 1) * LANES] = share(half, p) * factor

    for step in (1, 3):
        z_copy(step, own).wait_send()

    @pl.when(outer)
    def _():
        z_copy(2, own).wait_send()

    @pl.when(inner)
    def _():
        relay(own, z0).wait_send()

    for step in (1, 2, 3):
        x_copy(step, x0).wait_send()
        hour_copy(step, x0).wait_send()
        for h in range(2):
            for core in range(2):
                ref_copy(step, h, core, day).wait_send()
    for z in range(4):
        core_copy(z, c0).wait_send()
    for h in range(2):

        @pl.when(jnp.logical_not(jnp.logical_and(mine, h0 == h)))
        def _():
            for core in range(2):
                ref_copy(0, h, core, day).wait_send()


def write_out(hourly_ref, stack_ref, hourly_hbm, stack_hbm, sems):
    copies = [
        pltpu.make_async_copy(hourly_ref, hourly_hbm, sems.at[0]),
        pltpu.make_async_copy(stack_ref, stack_hbm, sems.at[1]),
    ]
    for copy in copies:
        copy.start()
    for copy in copies:
        copy.wait()


def on_device(spectra, flags, pair_mask):
    table = jnp.asarray(lag_table())
    bf16, f32 = jnp.bfloat16, jnp.float32
    dma = pltpu.SemaphoreType.DMA
    vmem = pltpu.VMEM
    operands = (jnp.transpose(spectra, (0, 1, 3, 2, 4)), flags, pair_mask, table)
    shapes = (
        jax.ShapeDtypeStruct((1, 9, 1, 32, LAGS), bf16),
        jax.ShapeDtypeStruct((9, 1, 4, LAGS), f32),
    )
    results = pl.pallas_call(
        kernel,
        out_shape=shapes,
        in_specs=[pl.BlockSpec(memory_space=pl.ANY)] * 4,
        out_specs=(
            pl.BlockSpec(memory_space=pltpu.VMEM),
            pl.BlockSpec(memory_space=pltpu.VMEM),
        ),
        scratch_shapes=[
            vmem((1, 2, 3, WIN, BINS), bf16),
            vmem((1, WIN), jnp.int32),
            vmem((1, 32), jnp.int32),
            vmem((8, BINS + PAD), f32),
            vmem((ROWS, LANES), f32),
            vmem((8, ROWS, LANES), bf16),
            vmem((4, ROWS, LANES), bf16),
            vmem((2 * ROWS, LANES), f32),
            vmem((8 * ROWS, LANES), f32),
            vmem((8 * ROWS, LANES), f32),
            vmem((2 * BINS, LAGS), bf16),
            vmem((4 * BLOCK, 2 * BINS), bf16),
            vmem((8 * BLOCK, LANES), f32),
            vmem((32, LANES), f32),
            vmem((8, LANES), f32),
            vmem((4, 2, 2, 48, LANES), bf16),
            vmem((4, 2, 2, 48, LANES), bf16),
            vmem((16, 48, LANES), bf16),
            vmem((4 * 128, LANES), f32),
            vmem((4 * 32, LANES), f32),
            vmem((BLOCK, LANES), f32),
            dma((3,)),
            dma,
            dma((4,)),
            dma((4,)),
            dma,
            dma((4,)),
            dma((4,)),
            dma((4,)),
            dma((4,)),
            dma((4,)),
            dma((4,)),
            dma((4, 2, 2)),
            dma((16,)),
            pltpu.SemaphoreType.REGULAR,
        ],
        compiler_params=pltpu.CompilerParams(
            collective_id=0, has_side_effects=True, vmem_limit_bytes=32 * 1024 * 1024
        ),
        cost_estimate=pl.CostEstimate(
            flops=500_000_000, bytes_accessed=2_000_000, transcendentals=6144
        ),
    )(*(pltpu.with_memory_space_constraint(a, pltpu.HBM) for a in operands))
    return pl.pallas_call(
        write_out,
        out_shape=shapes,
        in_specs=[pl.BlockSpec(memory_space=pltpu.VMEM)] * 2,
        out_specs=(pl.BlockSpec(memory_space=pl.ANY),) * 2,
        scratch_shapes=[dma((2,))],
        compiler_params=pltpu.CompilerParams(vmem_limit_bytes=1024 * 1024),
    )(*results)


def solution(mesh):
    placed = (P("sta", None, "day", None, None), P("sta", "day"), P("sta", None))
    return jax.shard_map(
        on_device,
        mesh=mesh,
        in_specs=placed,
        out_specs=(P("day", None, "sta", None, None), P(None, "sta", "day", None)),
        check_vma=False,
    )
```

```python
import math

import jax
import jax.numpy as jnp
import ml_dtypes
import numpy as np
from jax import lax
from jax.experimental import pallas as pl
from jax.experimental.pallas import tpu as pltpu
from jax.sharding import PartitionSpec as P

BINS = 1536
LAGS = 256
HALF_BAND = 16
WIN = 4
LANES = 128
FC = BINS // LANES
ROWS_FC = 24
FLAG_ROWS = 16
ROWS = FLAG_ROWS + FC * ROWS_FC
BLOCK = 80
PAD = 128
MESH = pl.DeviceIdType.MESH


def lag_table():
    freq = np.arange(BINS, dtype=np.int64)
    lag = np.arange(LAGS, dtype=np.int64) - LAGS // 2
    angle = (freq[:, None] * lag[None, :] % (2 * BINS)) * (math.pi / BINS)
    parts = np.stack([np.cos(angle), -np.sin(angle)]).reshape(2, FC, LANES, LAGS)
    rows = np.transpose(parts, (1, 0, 2, 3)).reshape(2 * BINS, LAGS)
    return rows.astype(np.float32).astype(ml_dtypes.bfloat16)


def kernel(
    spec_hbm, flags_hbm, mask_hbm, table_hbm,
    hourly_ref, stack_ref,
    spec_ref, flags_ref, mask_ref, power, white, t_blocks, s_blocks, t_wide, s_wide, s_tiles, table, products, totals,
    mask_col, mask_own, result, hour_recv, ref_recv, hour_wide, hour_rest, ref_wide,
    in_sems, table_sem, zs, zr, fs, xs, xr, cs, cr, hs, hr, rs, rr, ready,
):
    sta = lax.axis_index("sta")
    day = lax.axis_index("day")
    x0, z0, c0 = sta // 8, (sta // 2) % 4, sta % 2
    y0, h0 = day // 2, day % 2

    def sta_of(x, z, c):
        return (x * 4 + z) * 2 + c

    def at(x, z, c, d):
        return (sta_of(x, z, c), d)

    sibling = at(x0, z0, 1 - c0, day)

    barrier = pltpu.get_barrier_semaphore()

    def greet(target):
        pl.semaphore_signal(barrier, inc=1, device_id=target, device_id_type=MESH)

    for step in (3, 1, 2):
        greet(at(x0, (z0 + step) % 4, c0, day))
    for step in (2, 1, 3):
        greet(at((x0 + step) % 4, z0, c0, day))
    greet(sibling)
    mine = x0 == y0
    early = h0 == 0
    for y in range(4):

        @pl.when(y != y0)
        def _():
            greet(at(x0, z0, c0, y * 2 + h0))

        @pl.when(early)
        def _():
            greet(at(y0, z0, c0, y * 2 + 1))
            greet(at(y, z0, c0, x0 * 2 + 1))

    loads = [
        pltpu.make_async_copy(spec_hbm, spec_ref, in_sems.at[0]),
        pltpu.make_async_copy(flags_hbm, flags_ref, in_sems.at[1]),
        pltpu.make_async_copy(mask_hbm, mask_ref, in_sems.at[2]),
    ]
    for load in loads:
        load.start()
    table_copy = pltpu.make_async_copy(table_hbm, table, table_sem)
    table_copy.start()

    loads[0].wait()
    loads[1].wait()
    power[...] = jnp.zeros_like(power)
    energy = None
    for part in range(2):
        for comp in range(3):
            values = spec_ref[0, part, comp].astype(jnp.float32)
            energy = values * values if energy is None else energy + values * values
    power[0:WIN, 0:BINS] = energy
    single = power[...]
    span = single
    for shift in (1, 2, 4, 8, 16):
        span = span + pltpu.roll(span, shift, axis=1)
    span = span + pltpu.roll(single, 2 * HALF_BAND, axis=1)
    smooth = pltpu.roll(span, BINS + PAD - HALF_BAND, axis=1)[0:WIN, 0:BINS]
    line = lax.broadcasted_iota(jnp.int32, (WIN, WIN), 0)
    place = lax.broadcasted_iota(jnp.int32, (WIN, WIN), 1)
    spread = jnp.broadcast_to((1 - flags_ref[...]).astype(jnp.float32), (WIN, WIN))
    good = jnp.sum(jnp.where(line == place, spread, 0.0), axis=1, keepdims=True)
    scale = lax.rsqrt(smooth / (6.0 * (2 * HALF_BAND + 1)) + 1e-06) * good
    for part in range(2):
        for comp in range(3):
            y = spec_ref[0, part, comp].astype(jnp.float32) * scale
            first = FLAG_ROWS + (part * 3 + comp) * WIN
            for fc in range(FC):
                white[first + fc * ROWS_FC : first + fc * ROWS_FC + WIN, :] = y[
                    :, fc * LANES : (fc + 1) * LANES
                ]
    white[0:WIN, :] = jnp.broadcast_to(good, (WIN, LANES))
    white[WIN:FLAG_ROWS, :] = jnp.zeros((FLAG_ROWS - WIN, LANES), jnp.float32)
    block = white[...].astype(jnp.bfloat16)
    own = z0 * 2 + c0
    t_blocks[own] = block
    s_blocks[x0] = block

    loads[2].wait()
    spread = jnp.broadcast_to(mask_ref[...].astype(jnp.float32), (32, 32))
    line = lax.broadcasted_iota(jnp.int32, (32, 32), 0)
    place = lax.broadcasted_iota(jnp.int32, (32, 32), 1)
    column = jnp.sum(jnp.where(line == place, spread, 0.0), axis=1, keepdims=True)
    mask_col[...] = jnp.broadcast_to(column, (32, LANES))
    column = jnp.sum(
        jnp.where(line[0:8] + day * 4 == place[0:8], spread[0:8], 0.0), axis=1, keepdims=True
    )
    mask_own[...] = jnp.broadcast_to(column, (8, LANES))

    @pl.when(early)
    def _():
        pl.semaphore_wait(barrier, 10)

    @pl.when(jnp.logical_not(early))
    def _():
        pl.semaphore_wait(barrier, 18)
        for y in range(4):
            pl.semaphore_signal(
                ready, inc=1, device_id=at(y0, z0, c0, y * 2), device_id_type=MESH
            )


    def z_copy(step, slot):
        return pltpu.make_async_remote_copy(
            src_ref=t_blocks.at[own],
            dst_ref=t_blocks.at[slot],
            send_sem=zs.at[step],
            recv_sem=zr.at[step],
            device_id=at(x0, (z0 + step) % 4, c0, day),
            device_id_type=MESH,
        )

    def relay(slot, z):
        return pltpu.make_async_remote_copy(
            src_ref=t_blocks.at[slot],
            dst_ref=t_blocks.at[slot],
            send_sem=fs,
            recv_sem=zr.at[2],
            device_id=at(x0, z, c0, day),
            device_id_type=MESH,
        )

    def x_copy(step, slot):
        return pltpu.make_async_remote_copy(
            src_ref=s_blocks.at[x0],
            dst_ref=s_blocks.at[slot],
            send_sem=xs.at[step],
            recv_sem=xr.at[step],
            device_id=at((x0 + step) % 4, z0, c0, day),
            device_id_type=MESH,
        )

    outer = jnp.logical_or(z0 == 0, z0 == 3)
    inner = jnp.logical_not(outer)
    def core_copy(z, core):
        slot = z * 2 + core
        return pltpu.make_async_remote_copy(
            src_ref=t_blocks.at[slot],
            dst_ref=t_blocks.at[slot],
            send_sem=cs.at[z],
            recv_sem=cr.at[z],
            device_id=sibling,
            device_id_type=MESH,
        )

    @pl.when(z0 == 0)
    def _():
        z_copy(1, own).start()

    z_copy(3, own).start()

    @pl.when(z0 > 0)
    def _():
        z_copy(1, own).start()

    for step in (2, 1, 3):
        x_copy(step, x0).start()

    @pl.when(outer)
    def _():
        z_copy(2, own).start()

    core_copy(z0, c0).start()

    def arrive(z):
        z_copy((z0 - z + 4) % 4, z * 2 + c0).wait_recv()
        core_copy(z, c0).start()

    high_rows = lax.broadcasted_iota(jnp.int32, (8, LANES), 0) >= 4

    def t_tile(row):
        first = jnp.broadcast_to(t_wide[pl.ds(row, 1), :], (8, LANES))
        second = jnp.broadcast_to(t_wide[pl.ds(ROWS + row, 1), :], (8, LANES))
        return jnp.where(high_rows, second, first)

    def s_tile(row):
        return s_tiles[pl.ds(pl.multiple_of(row * 8, 8), 8), :]

    def cross(h, core):
        for bit in range(2):
            t_wide[bit * ROWS : (bit + 1) * ROWS, :] = t_blocks[(2 * h + bit) * 2 + core].astype(
                jnp.float32
            )

        def chunk(fc, carry):
            base = FLAG_ROWS + fc * ROWS_FC
            local = [s_tile(base + r) for r in range(ROWS_FC)]
            column = pl.multiple_of(fc * 2 * LANES, 2 * LANES)
            re_tiles, im_tiles = [None] * 9, [None] * 9
            for b in range(3):
                other = [
                    t_tile(base + (part * 3 + b) * WIN + w) for part in range(2) for w in range(WIN)
                ]
                for a in range(3):
                    re, im = None, None
                    for w in range(WIN):
                        s_re, s_im = local[a * WIN + w], local[(3 + a) * WIN + w]
                        t_re, t_im = other[w], other[WIN + w]
                        re_term = s_re * t_re + s_im * t_im
                        im_term = s_im * t_re - s_re * t_im
                        re = re_term if re is None else re + re_term
                        im = im_term if im is None else im + im_term
                    re_tiles[a * 3 + b] = re
                    im_tiles[a * 3 + b] = im
            rows = pl.ds(pl.multiple_of((2 * h + core) * BLOCK, 16), BLOCK)
            zero = jnp.zeros((8, LANES), jnp.float32)
            products[rows, pl.ds(column, LANES)] = jnp.concatenate(
                re_tiles + [zero], axis=0
            ).astype(jnp.bfloat16)
            products[rows, pl.ds(column + LANES, LANES)] = jnp.concatenate(
                im_tiles + [zero], axis=0
            ).astype(jnp.bfloat16)
            return carry

        lax.fori_loop(0, FC, chunk, 0)
        count = None
        for w in range(WIN):
            g = s_tile(w) * t_tile(w)
            count = g if count is None else count + g
        for half in range(2):
            first = (4 * half + 2 * h + core) * BLOCK + 72
            totals[pl.ds(pl.multiple_of(first, 8), 8), :] = count

    def transform(h, core):
        term = jnp.dot(
            products[pl.ds(pl.multiple_of((2 * h + core) * BLOCK, 16), BLOCK), :],
            table[...],
            preferred_element_type=jnp.float32,
        ) * (1.0 / math.sqrt(BINS))
        for half in range(2):
            first = pl.multiple_of((4 * half + 2 * h + core) * BLOCK, 8)
            totals[pl.ds(first, 72), :] = term[0:72, half * LANES : (half + 1) * LANES]

    def hour_copy(step, slot):
        return pltpu.make_async_remote_copy(
            src_ref=result.at[step],
            dst_ref=hour_recv.at[slot],
            send_sem=hs.at[step],
            recv_sem=hr.at[step],
            device_id=at((x0 + step) % 4, z0, c0, day),
            device_id_type=MESH,
        )

    def ref_copy(step, h, core, d):
        slot = core * 8 + d
        return pltpu.make_async_remote_copy(
            src_ref=result.at[step, core, h],
            dst_ref=ref_recv.at[slot],
            send_sem=rs.at[step, h, core],
            recv_sem=rr.at[slot],
            device_id=at((x0 + step) % 4, z0, c0, x0 * 2 + h),
            device_id_type=MESH,
        )

    def send_share(h, core):
        for step in (2, 1, 3, 0):
            x = (x0 + step) % 4
            starts = [
                (4 * half + 2 * h + core) * BLOCK + bit * 4 + x
                for bit in range(2)
                for half in range(2)
            ]
            tiles = [totals[pl.ds(first, 8, stride=8), :] for first in starts]
            rest = [totals[pl.ds(first + 64, 2, stride=8), :] for first in starts]
            zero = jnp.zeros((8, LANES), jnp.float32)
            result[step, core, h] = jnp.concatenate(tiles + rest + [zero], axis=0).astype(
                jnp.bfloat16
            )
            now = jnp.logical_or(jnp.logical_not(early), h == 0)
            if step == 0:
                local = jnp.logical_and(mine, h0 == h)

                @pl.when(local)
                def _():
                    ref_recv[core * 8 + day] = result[0, core, h]

                now = jnp.logical_and(now, jnp.logical_not(local))

            @pl.when(now)
            def _():
                ref_copy(step, h, core, day).start()

    @pl.when(outer)
    def _():
        arrive(1 + z0 // 3)

    @pl.when(z0 == 1)
    def _():
        arrive(0)

    @pl.when(inner)
    def _():
        arrive(3 - z0)
        relay((3 - z0) * 2 + c0, 3 * (z0 - 1)).start()

    for step in (1, 3, 2):
        x_copy(step, (x0 - step + 4) % 4).wait_recv()
    for slot in range(4):
        values = s_blocks[slot].astype(jnp.float32)
        s_wide[slot * ROWS : (slot + 1) * ROWS, :] = values
        s_wide[(4 + slot) * ROWS : (5 + slot) * ROWS, :] = values

    def prepare(i, carry):
        for r in range(16):
            row = i * 16 + r
            s_tiles[pl.ds(pl.multiple_of(row * 8, 8), 8), :] = s_wide[
                pl.ds(row, 8, stride=ROWS), :
            ]
        return carry

    lax.fori_loop(0, ROWS // 16, prepare, 0)
    def part(h, core):
        cross(h, core)
        transform(h, core)
        send_share(h, core)

    table_copy.wait()

    @pl.when(z0 >= 2)
    def _():
        arrive(0)

    @pl.when(z0 == 3)
    def _():
        arrive(1)

    part(0, c0)
    core_copy(0, 1 - c0).wait_recv()
    core_copy(1, 1 - c0).wait_recv()
    part(0, 1 - c0)

    @pl.when(z0 < 3)
    def _():
        arrive(3)

    @pl.when(z0 == 0)
    def _():
        arrive(2)

    cross(1, c0)

    core_copy(2, 1 - c0).wait_recv()
    core_copy(3, 1 - c0).wait_recv()
    transform(1, c0)
    send_share(1, c0)
    part(1, 1 - c0)

    for step in (2, 1, 3):
        hour_copy(step, x0).start()
    hour_recv[x0] = result[0]

    @pl.when(early)
    def _():
        pl.semaphore_wait(ready, 4)
        for step in (2, 1, 3, 0):
            for core in range(2):
                ref_copy(step, 1, core, day).start()

    for step in (1, 3, 2):
        hour_copy(step, (x0 - step + 4) % 4).wait_recv()
    for x in range(4):
        for core in range(2):
            for h in range(2):
                got = hour_recv[x, core, h].astype(jnp.float32)
                for bit in range(2):
                    for half in range(2):
                        tile = bit * 2 + half
                        t = (h * 2 + bit) * 2 + core
                        first = x * 128 + t * 16 + half * 8
                        hour_wide[first : first + 8, :] = got[tile * 8 : tile * 8 + 8]
                        first = x * 32 + t * 4 + half * 2
                        hour_rest[first : first + 2, :] = got[32 + tile * 2 : 34 + tile * 2]

    def hour_tile(x, half, p):
        if p < 8:
            return hour_wide[pl.ds(x * 128 + half * 8 + p, 8, stride=16), :]
        return hour_rest[pl.ds(x * 32 + half * 2 + p - 8, 8, stride=4), :]

    for pair in range(2):
        for half in range(2):
            factors = [
                mask_col[x * 8 : x * 8 + 8, :] / jnp.maximum(hour_tile(x, half, 9), 1.0)
                for x in (pair * 2, pair * 2 + 1)
            ]
            for p in range(9):
                tiles = [hour_tile(pair * 2 + i, half, p) * factors[i] for i in range(2)]
                hourly_ref[
                    0, p, 0, pair * 16 : pair * 16 + 16, half * LANES : (half + 1) * LANES
                ] = jnp.concatenate(tiles, axis=0).astype(jnp.bfloat16)

    for core in range(2):
        for d in range(8):

            @pl.when(jnp.logical_not(jnp.logical_and(mine, day == d)))
            def _():
                ref_copy(1, 0, core, d).wait_recv()

    for core in range(2):
        summed = ref_recv[core * 8].astype(jnp.float32)
        for d in range(1, 8):
            summed = summed + ref_recv[core * 8 + d].astype(jnp.float32)
        for bit in range(2):
            for half in range(2):
                tile = bit * 2 + half
                first = (bit * 2 + core) * 16 + half * 8
                ref_wide[first : first + 8, :] = summed[tile * 8 : tile * 8 + 8]
                first = 64 + (bit * 2 + core) * 4 + half * 2
                ref_wide[first : first + 2, :] = summed[32 + tile * 2 : 34 + tile * 2]

    def share(half, p):
        if p < 8:
            return ref_wide[pl.ds(half * 8 + p, 4, stride=16), :]
        return ref_wide[pl.ds(64 + half * 2 + p - 8, 4, stride=4), :]

    for half in range(2):
        factor = mask_own[0:4, :] / jnp.maximum(share(half, 9), 1.0)
        for p in range(9):
            stack_ref[p, 0, :, half * LANES : (half + 1) * LANES] = share(half, p) * factor

    for step in (1, 3):
        z_copy(step, own).wait_send()

    @pl.when(outer)
    def _():
        z_copy(2, own).wait_send()

    @pl.when(inner)
    def _():
        relay(own, z0).wait_send()

    for step in (1, 2, 3):
        x_copy(step, x0).wait_send()
        hour_copy(step, x0).wait_send()
        for h in range(2):
            for core in range(2):
                ref_copy(step, h, core, day).wait_send()
    for z in range(4):
        core_copy(z, c0).wait_send()
    for h in range(2):

        @pl.when(jnp.logical_not(jnp.logical_and(mine, h0 == h)))
        def _():
            for core in range(2):
                ref_copy(0, h, core, day).wait_send()


def write_out(hourly_ref, stack_ref, hourly_hbm, stack_hbm, sems):
    copies = [
        pltpu.make_async_copy(hourly_ref, hourly_hbm, sems.at[0]),
        pltpu.make_async_copy(stack_ref, stack_hbm, sems.at[1]),
    ]
    for copy in copies:
        copy.start()
    for copy in copies:
        copy.wait()


def on_device(spectra, flags, pair_mask):
    table = jnp.asarray(lag_table())
    bf16, f32 = jnp.bfloat16, jnp.float32
    dma = pltpu.SemaphoreType.DMA
    vmem = pltpu.VMEM
    operands = (jnp.transpose(spectra, (0, 1, 3, 2, 4)), flags, pair_mask, table)
    shapes = (
        jax.ShapeDtypeStruct((1, 9, 1, 32, LAGS), bf16),
        jax.ShapeDtypeStruct((9, 1, 4, LAGS), f32),
    )
    results = pl.pallas_call(
        kernel,
        out_shape=shapes,
        in_specs=[pl.BlockSpec(memory_space=pl.ANY)] * 4,
        out_specs=(
            pl.BlockSpec(memory_space=pltpu.VMEM),
            pl.BlockSpec(memory_space=pltpu.VMEM),
        ),
        scratch_shapes=[
            vmem((1, 2, 3, WIN, BINS), bf16),
            vmem((1, WIN), jnp.int32),
            vmem((1, 32), jnp.int32),
            vmem((8, BINS + PAD), f32),
            vmem((ROWS, LANES), f32),
            vmem((8, ROWS, LANES), bf16),
            vmem((4, ROWS, LANES), bf16),
            vmem((2 * ROWS, LANES), f32),
            vmem((8 * ROWS, LANES), f32),
            vmem((8 * ROWS, LANES), f32),
            vmem((2 * BINS, LAGS), bf16),
            vmem((4 * BLOCK, 2 * BINS), bf16),
            vmem((8 * BLOCK, LANES), f32),
            vmem((32, LANES), f32),
            vmem((8, LANES), f32),
            vmem((4, 2, 2, 48, LANES), bf16),
            vmem((4, 2, 2, 48, LANES), bf16),
            vmem((16, 48, LANES), bf16),
            vmem((4 * 128, LANES), f32),
            vmem((4 * 32, LANES), f32),
            vmem((BLOCK, LANES), f32),
            dma((3,)),
            dma,
            dma((4,)),
            dma((4,)),
            dma,
            dma((4,)),
            dma((4,)),
            dma((4,)),
            dma((4,)),
            dma((4,)),
            dma((4,)),
            dma((4, 2, 2)),
            dma((16,)),
            pltpu.SemaphoreType.REGULAR,
        ],
        compiler_params=pltpu.CompilerParams(
            collective_id=0, has_side_effects=True, vmem_limit_bytes=32 * 1024 * 1024
        ),
        cost_estimate=pl.CostEstimate(
            flops=500_000_000, bytes_accessed=2_000_000, transcendentals=6144
        ),
    )(*(pltpu.with_memory_space_constraint(a, pltpu.HBM) for a in operands))
    return pl.pallas_call(
        write_out,
        out_shape=shapes,
        in_specs=[pl.BlockSpec(memory_space=pltpu.VMEM)] * 2,
        out_specs=(pl.BlockSpec(memory_space=pl.ANY),) * 2,
        scratch_shapes=[dma((2,))],
        compiler_params=pltpu.CompilerParams(vmem_limit_bytes=1024 * 1024),
    )(*results)


def solution(mesh):
    placed = (P("sta", None, "day", None, None), P("sta", "day"), P("sta", None))
    return jax.shard_map(
        on_device,
        mesh=mesh,
        in_specs=placed,
        out_specs=(P("day", None, "sta", None, None), P(None, "sta", "day", None)),
        check_vma=False,
    )
```
